128 devices in a mesh: fsdp: 8 (over x, z_hi), ctx: 16 (over z_lo, y, core).
Axes of the slice: x: 4, y: 4, z: 4 (z_hi: 2, z_lo: 2; z = z_hi * 2 + z_lo), core: 2. Of those that a mesh axis runs over, the one named last changes fastest.
Arguments:
- inputs: bfloat16 [65536, 640], P(('fsdp', 'ctx')), may hold values from -6 to 6
- cotangent: bfloat16 [65536, 640], P(('fsdp', 'ctx')), may hold values from -6 to 6
- query_weight: float32 [640, 1024], P(None, ('fsdp', 'ctx')), may hold values from -0.25 to 0.25
- key_weight: float32 [640, 256], P(('fsdp', 'ctx')), may hold values from -0.25 to 0.25
- value_weight: float32 [640, 256], P(('fsdp', 'ctx')), may hold values from -0.25 to 0.25
- output_weight: float32 [1024, 640], P(('fsdp', 'ctx')), may hold values from -0.375 to 0.375
- gate_weight: float32 [640, 2048], P(None, ('fsdp', 'ctx')), may hold values from -0.25 to 0.25
- up_weight: float32 [640, 2048], P(None, ('fsdp', 'ctx')), may hold values from -0.25 to 0.25
- down_weight: float32 [2048, 640], P(('fsdp', 'ctx')), may hold values from -0.125 to 0.125
- norm_gains: float32 [2, 640], P(None, ('fsdp', 'ctx')), may hold values from 0.5 to 1.5
- query_moment: float32 [640, 1024], P(None, ('fsdp', 'ctx')), may hold values from -614.4 to 614.4
- key_moment: float32 [640, 256], P(('fsdp', 'ctx')), may hold values from -1228.8 to 1228.8
- value_moment: float32 [640, 256], P(('fsdp', 'ctx')), may hold values from -1638.4 to 1638.4
- output_moment: float32 [1024, 640], P(('fsdp', 'ctx')), may hold values from -1638.4 to 1638.4
- gate_moment: float32 [640, 2048], P(None, ('fsdp', 'ctx')), may hold values from -2048 to 2048
- up_moment: float32 [640, 2048], P(None, ('fsdp', 'ctx')), may hold values from -2048 to 2048
- down_moment: float32 [2048, 640], P(('fsdp', 'ctx')), may hold values from -2457.6 to 2457.6
- gain_first: float32 [2, 640], P(None, ('fsdp', 'ctx')), may hold values from -115.2 to 115.2
- gain_second: float32 [2, 640], P(None, ('fsdp', 'ctx')), may hold values from 5.89824 to 262.144, as said below
Outputs:
- block_output: float32 [65536, 640], P(('fsdp', 'ctx'))
- input_grad: float32 [65536, 640], P(('fsdp', 'ctx'))
- query_grad: float32 [640, 1024], P(None, ('fsdp', 'ctx'))
- key_grad: float32 [640, 256], P(('fsdp', 'ctx'))
- value_grad: float32 [640, 256], P(('fsdp', 'ctx'))
- output_grad: float32 [1024, 640], P(('fsdp', 'ctx'))
- gate_grad: float32 [640, 2048], P(None, ('fsdp', 'ctx'))
- up_grad: float32 [640, 2048], P(None, ('fsdp', 'ctx'))
- down_grad: float32 [2048, 640], P(('fsdp', 'ctx'))
- query_momentum: float32 [640, 1024], P(None, ('fsdp', 'ctx'))
- key_momentum: float32 [640, 256], P(('fsdp', 'ctx'))
- value_momentum: float32 [640, 256], P(('fsdp', 'ctx'))
- output_momentum: float32 [1024, 640], P(('fsdp', 'ctx'))
- gate_momentum: float32 [640, 2048], P(None, ('fsdp', 'ctx'))
- up_momentum: float32 [640, 2048], P(None, ('fsdp', 'ctx'))
- down_momentum: float32 [2048, 640], P(('fsdp', 'ctx'))
- query_updated: float32 [640, 1024], P(None, ('fsdp', 'ctx'))
- key_updated: float32 [640, 256], P(('fsdp', 'ctx'))
- value_updated: float32 [640, 256], P(('fsdp', 'ctx'))
- output_updated: float32 [1024, 640], P(('fsdp', 'ctx'))
- gate_updated: float32 [640, 2048], P(None, ('fsdp', 'ctx'))
- up_updated: float32 [640, 2048], P(None, ('fsdp', 'ctx'))
- down_updated: float32 [2048, 640], P(('fsdp', 'ctx'))
- gain_grads: float32 [2, 640], P(None, ('fsdp', 'ctx'))
- first_moments: float32 [2, 640], P(None, ('fsdp', 'ctx'))
- second_moments: float32 [2, 640], P(None, ('fsdp', 'ctx'))
- gains_updated: float32 [2, 640], P(None, ('fsdp', 'ctx'))
The draws below stay inside these ranges and needn't reach their ends.
Inputs may be any that keep to these rules, and one draw needn't show every extreme that they name: `gain_second`: positive.
All inputs are finite; a program needn't handle non-finite values.
Results may differ from the reference program's by a relative error of at most 0.013.
The reference program's roundings to bfloat16 on the way count: a program that leaves them out, or rounds other values in their place, can miss the bound.
Values may be sent and summed in bfloat16 or wider, within the bound.
A program may use at most 192 MiB of HBM per device.

```python
import math
import jax
import jax.numpy as jnp
from jax import lax

D = 640
HQ = 4
HD = 256
FF = 2048
WINDOW = 512
NS_ITERS = 4
ADAM_STEP = 10
TOKENS = 65536
LENGTH = 8192
SEQS = 8


def shaped(entries, key, shard_dim, factor, rise, other_high):
    row_count, col_count = entries.shape
    along = row_count if shard_dim == 0 else col_count
    across = col_count if shard_dim == 0 else row_count
    key_jitter, key_across = jax.random.split(key)
    position = jnp.arange(along, dtype=jnp.float32) / along
    jitter = jax.random.uniform(key_jitter, (along,), jnp.float32, 0.8, 1.25)
    rising = jnp.exp(math.log(rise) * position) * jitter
    spread_across = jnp.exp(jax.random.uniform(key_across, (across,), jnp.float32, 0.0, math.log(other_high)))
    divisor = math.sqrt((rise * rise - 1.0) / (2.0 * math.log(rise))) * math.sqrt((other_high * other_high - 1.0) / (2.0 * math.log(other_high)))
    if shard_dim == 0:
        profile = rising[:, None] * spread_across[None, :]
    else:
        profile = spread_across[:, None] * rising[None, :]
    return entries * profile * (factor * math.sqrt(TOKENS) / divisor)


def draw_query_moment(key, part):
    key = jax.random.fold_in(key, 11)
    key_base, key_shape = jax.random.split(key)
    entries = jax.random.truncated_normal(key_base, -4.0, 4.0, (D, HQ * HD), jnp.float32)
    return shaped(entries, key_shape, 1, 0.15, 6.0, 3.0)


def draw_key_moment(key, part):
    key = jax.random.fold_in(key, 12)
    key_base, key_shape = jax.random.split(key)
    entries = jax.random.truncated_normal(key_base, -4.0, 4.0, (D, HD), jnp.float32)
    return shaped(entries, key_shape, 0, 0.3, 6.0, 3.0)


def draw_value_moment(key, part):
    key = jax.random.fold_in(key, 13)
    key_base, key_shape = jax.random.split(key)
    entries = jax.random.truncated_normal(key_base, -4.0, 4.0, (D, HD), jnp.float32)
    return shaped(entries, key_shape, 0, 0.4, 6.0, 3.0)


def draw_output_moment(key, part):
    key = jax.random.fold_in(key, 14)
    key_base, key_shape = jax.random.split(key)
    entries = jax.random.truncated_normal(key_base, -4.0, 4.0, (HQ * HD, D), jnp.float32)
    return shaped(entries, key_shape, 0, 0.4, 6.0, 3.0)


def draw_gate_moment(key, part):
    key = jax.random.fold_in(key, 15)
    key_base, key_shape = jax.random.split(key)
    entries = jax.random.truncated_normal(key_base, -4.0, 4.0, (D, FF), jnp.float32)
    return shaped(entries, key_shape, 1, 0.5, 6.0, 3.0)


def draw_up_moment(key, part):
    key = jax.random.fold_in(key, 16)
    key_base, key_shape = jax.random.split(key)
    entries = jax.random.truncated_normal(key_base, -4.0, 4.0, (D, FF), jnp.float32)
    return shaped(entries, key_shape, 1, 0.5, 6.0, 3.0)


def draw_down_moment(key, part):
    key = jax.random.fold_in(key, 17)
    key_base, key_shape = jax.random.split(key)
    entries = jax.random.truncated_normal(key_base, -4.0, 4.0, (FF, D), jnp.float32)
    return shaped(entries, key_shape, 0, 0.6, 6.0, 3.0)


def draw_gain_first(key, part):
    key = jax.random.fold_in(key, 21)
    row_scales = jnp.array([[0.3], [1.0]], jnp.float32) * (0.111 * math.sqrt(TOKENS))
    entries = jax.random.truncated_normal(key, -4.0, 4.0, (2, D), jnp.float32)
    return entries * row_scales


def draw_gain_second(key, part):
    key = jax.random.fold_in(key, 22)
    row_scales = jnp.array([[0.09], [1.0]], jnp.float32) * (0.001 * TOKENS)
    factors = jnp.exp(jax.random.uniform(key, (2, D), jnp.float32, 0.0, math.log(4.0)))
    return factors * row_scales


def steps_of(own_key, extent, shards, low, top_value):
    gain, own = 1.0, jax.random.fold_in(own_key, 6)
    for dim, parts in shards:
        steps = jnp.exp(jax.random.uniform(jax.random.fold_in(own, dim), (parts,), jnp.float32, low / len(shards), top_value / len(shards)))
        gain = gain * jnp.repeat(steps, extent[dim] // parts).reshape([-1 if axis == dim else 1 for axis in range(len(extent))])
    return gain


def centred(own_key, shape, width, reach, pieces=(), kind=jnp.bfloat16):
    values = jax.random.normal(own_key, shape, jnp.float32) * width
    if len(pieces) > 0:
        values = steps_of(own_key, shape, pieces, -0.22, 0.18) * values
    return jnp.clip(values, min=-reach, max=reach).astype(kind)


def setup_inputs(seed: int = 0) -> dict:
    arg_keys = jax.random.split(jax.random.key(seed), 20)
    return {
        "inputs": centred(arg_keys[0], (TOKENS, D), 1.0, 6.0, ((0, 128),)),
        "cotangent": centred(arg_keys[1], (TOKENS, D), 1.0, 6.0, ((0, 128),)),
        "query_weight": centred(arg_keys[2], (D, HQ * HD), D ** -0.5, 0.25, ((1, 128),), jnp.float32),
        "key_weight": centred(arg_keys[3], (D, HD), D ** -0.5, 0.25, ((0, 128),), jnp.float32),
        "value_weight": centred(arg_keys[4], (D, HD), D ** -0.5, 0.25, ((0, 128),), jnp.float32),
        "output_weight": centred(arg_keys[5], (HQ * HD, D), (HQ * HD // 4) ** -0.5, 0.375, ((0, 128),), jnp.float32),
        "gate_weight": centred(arg_keys[6], (D, FF), D ** -0.5, 0.25, ((1, 128),), jnp.float32),
        "up_weight": centred(arg_keys[7], (D, FF), D ** -0.5, 0.25, ((1, 128),), jnp.float32),
        "down_weight": centred(arg_keys[8], (FF, D), FF ** -0.5, 0.125, ((0, 128),), jnp.float32),
        "norm_gains": jnp.clip(1.0 + 0.1 * jax.random.normal(arg_keys[9], (2, D), jnp.float32), 0.5, 1.5),
        "query_moment": draw_query_moment(jax.random.fold_in(arg_keys[19], 71), 0),
        "key_moment": draw_key_moment(jax.random.fold_in(arg_keys[19], 71), 0),
        "value_moment": draw_value_moment(jax.random.fold_in(arg_keys[19], 71), 0),
        "output_moment": draw_output_moment(jax.random.fold_in(arg_keys[19], 71), 0),
        "gate_moment": draw_gate_moment(jax.random.fold_in(arg_keys[19], 71), 0),
        "up_moment": draw_up_moment(jax.random.fold_in(arg_keys[19], 71), 0),
        "down_moment": draw_down_moment(jax.random.fold_in(arg_keys[19], 71), 0),
        "gain_first": draw_gain_first(jax.random.fold_in(arg_keys[19], 71), 0),
        "gain_second": draw_gain_second(jax.random.fold_in(arg_keys[19], 71), 0),
    }


@jax.custom_vjp
def low(v):
    return lax.optimization_barrier(v.astype(jnp.bfloat16)).astype(jnp.float32)

@jax.custom_vjp
def low_back(v):
    return v

def low_keep(v):
    return (low(v), None)

def low_pass(kept, grad):
    return (grad,)

def back_keep(v):
    return (v, None)

def back_low(kept, grad):
    return (low(grad),)
low.defvjp(low_keep, low_pass)
low_back.defvjp(back_keep, back_low)
HIGH = lax.Precision.HIGHEST
NORM_EPS = 1e-06
ORTHO_EPS = 1e-07
POLY_FIRST = 3.4445
POLY_SECOND = -4.775
POLY_THIRD = 2.0315
MOMENTUM = 0.95
MUON_RATE = 0.6
MUON_DECAY = 0.01
ADAM_RATE = 0.7
BETA_FIRST = 0.9
BETA_SECOND = 0.999
ADAM_EPS = 1e-08

def rms_scale(values, gain_row):
    mean_square = lax.optimization_barrier(jnp.mean(values * values, axis=-1, keepdims=True))
    return values * lax.rsqrt(mean_square + NORM_EPS) * gain_row

def attention_sequence(packed):
    query_seq, key_seq, value_seq = packed
    length_here = query_seq.shape[0]
    block_rows = math.gcd(length_here, 512)
    pad_rows = jnp.zeros((WINDOW, HD), jnp.float32)
    key_padded = jnp.concatenate([pad_rows, key_seq], axis=0)
    value_padded = jnp.concatenate([pad_rows, value_seq], axis=0)
    score_scale = 1.0 / math.sqrt(HD)

    @jax.checkpoint
    def one_block(start_row):
        query_rows = lax.dynamic_slice_in_dim(query_seq, start_row, block_rows, 0)
        key_rows = lax.dynamic_slice_in_dim(key_padded, start_row, block_rows + WINDOW, 0)
        value_rows = lax.dynamic_slice_in_dim(value_padded, start_row, block_rows + WINDOW, 0)
        scores = jnp.einsum('ihd,jd->hij', query_rows, key_rows, precision=HIGH) * score_scale
        scores = low_back(scores)
        query_position = start_row + jnp.arange(block_rows, dtype=jnp.int32)
        key_position = start_row - WINDOW + jnp.arange(block_rows + WINDOW, dtype=jnp.int32)
        allowed = (key_position[None, :] <= query_position[:, None]) & (key_position[None, :] > query_position[:, None] - WINDOW) & (key_position[None, :] >= 0)
        masked = jnp.where(allowed[None], scores, -jnp.inf)
        row_max = lax.optimization_barrier(jnp.max(masked, axis=-1, keepdims=True))
        exp_scores = jnp.exp(masked - row_max)
        probabilities = low(exp_scores / lax.optimization_barrier(jnp.sum(exp_scores, axis=-1, keepdims=True)))
        return jnp.einsum('hij,jd->ihd', probabilities, value_rows, precision=HIGH)
    starts = (jnp.arange(length_here // block_rows, dtype=jnp.int32) * block_rows).astype(jnp.int32)
    blocks = lax.map(one_block, starts)
    return blocks.reshape(length_here, HQ, HD)

def forward(inputs, query_weight, key_weight, value_weight, output_weight, gate_weight, up_weight, down_weight, norm_gains):
    gains_low = low(norm_gains)
    first_normed = low(rms_scale(inputs, gains_low[0]))
    queries = low(low_back(jnp.dot(first_normed, low(query_weight), precision=HIGH)))
    key_values = low(low_back(jnp.dot(first_normed, low(key_weight), precision=HIGH)))
    value_values = low(low_back(jnp.dot(first_normed, low(value_weight), precision=HIGH)))
    attended = lax.map(attention_sequence, (queries.reshape(SEQS, LENGTH, HQ, HD), key_values.reshape(SEQS, LENGTH, HD), value_values.reshape(SEQS, LENGTH, HD)))
    attended = low(low_back(attended.reshape(TOKENS, HQ * HD)))
    branch_out = low_back(jnp.dot(attended, low(output_weight), precision=HIGH))
    middle = inputs + branch_out
    second_normed = low(rms_scale(middle, gains_low[1]))
    gate_values = low_back(jnp.dot(second_normed, low(gate_weight), precision=HIGH))
    up_values = low_back(jnp.dot(second_normed, low(up_weight), precision=HIGH))
    hidden = low(jax.nn.gelu(gate_values, approximate=True) * up_values)
    return middle + jnp.dot(hidden, low(down_weight), precision=HIGH)

def orthogonalize(moment, is_tall):
    norm_value = jnp.sqrt(jnp.sum(moment * moment))
    current = moment / (norm_value + ORTHO_EPS)
    for iteration in range(NS_ITERS):
        if is_tall:
            gram_matrix = jnp.dot(current.T, current, precision=HIGH)
            product = jnp.dot(current, gram_matrix, precision=HIGH)
            current = POLY_FIRST * current + POLY_SECOND * product + POLY_THIRD * jnp.dot(product, gram_matrix, precision=HIGH)
        else:
            gram_matrix = jnp.dot(current, current.T, precision=HIGH)
            product = jnp.dot(gram_matrix, current, precision=HIGH)
            current = POLY_FIRST * current + POLY_SECOND * product + POLY_THIRD * jnp.dot(gram_matrix, product, precision=HIGH)
    return current

def reference(inputs, cotangent, query_weight, key_weight, value_weight, output_weight, gate_weight, up_weight, down_weight, norm_gains, query_moment, key_moment, value_moment, output_moment, gate_moment, up_moment, down_moment, gain_first, gain_second):
    block_output, pullback = jax.vjp(forward, inputs.astype(jnp.float32), query_weight, key_weight, value_weight, output_weight, gate_weight, up_weight, down_weight, norm_gains)
    gradients = pullback(cotangent.astype(jnp.float32))
    masters = (query_weight, key_weight, value_weight, output_weight, gate_weight, up_weight, down_weight)
    moments = (query_moment, key_moment, value_moment, output_moment, gate_moment, up_moment, down_moment)
    tall_flags = (False, True, True, True, False, False, True)
    momenta = []
    updated = []
    for matrix_index in range(7):
        fresh = MOMENTUM * moments[matrix_index] + gradients[matrix_index + 1]
        orthogonal = orthogonalize(fresh, tall_flags[matrix_index])
        row_count, col_count = masters[matrix_index].shape
        step_ratio = math.sqrt(max(row_count, col_count) / row_count)
        momenta.append(fresh)
        updated.append(masters[matrix_index] * (1.0 - MUON_RATE * MUON_DECAY) - MUON_RATE * step_ratio * orthogonal)
    gain_grads = gradients[8]
    first_moments = BETA_FIRST * gain_first + (1.0 - BETA_FIRST) * gain_grads
    second_moments = BETA_SECOND * gain_second + (1.0 - BETA_SECOND) * gain_grads * gain_grads
    first_hat = first_moments / (1.0 - BETA_FIRST ** ADAM_STEP)
    second_hat = second_moments / (1.0 - BETA_SECOND ** ADAM_STEP)
    gains_updated = norm_gains - ADAM_RATE * first_hat / (jnp.sqrt(second_hat) + ADAM_EPS)
    return (block_output, gradients[0], gradients[1], gradients[2], gradients[3], gradients[4], gradients[5], gradients[6], gradients[7], momenta[0], momenta[1], momenta[2], momenta[3], momenta[4], momenta[5], momenta[6], updated[0], updated[1], updated[2], updated[3], updated[4], updated[5], updated[6], gain_grads, first_moments, second_moments, gains_updated)
```

```python
import itertools
import math

import jax
import jax.numpy as jnp
import numpy as np
from jax import lax
from jax.experimental import pallas as pl
from jax.experimental.pallas import tpu as pltpu
from jax.sharding import PartitionSpec as P

HQ = 4
HD = 256
D = 640
FF = 2048
WINDOW = 512
NS_ITERS = 4
ADAM_STEP = 10
DEVICES = 128

NORM_EPS = 1e-06
ORTHO_EPS = 1e-07
POLY_FIRST = 3.4445
POLY_SECOND = -4.775
POLY_THIRD = 2.0315
MOMENTUM = 0.95
MUON_RATE = 0.6
MUON_DECAY = 0.01
ADAM_RATE = 0.7
BETA_FIRST = 0.9
BETA_SECOND = 0.999
ADAM_EPS = 1e-08

AXES = ("fsdp", "ctx")
MESH = pl.DeviceIdType.MESH
ALL = slice(None)
BF = jnp.bfloat16
F32 = jnp.float32

CORE = 6
WIDTHS = (3 * D, D + HD)
CUBES = ((1, 5, 3), (0, 2, 4))
PIECES = (
    (1, 0, 256, 0, 0),
    (1, 256, 128, 0, 1),
    (1, 384, 128, 0, 2),
    (1, 512, 128, 1, 0),
    (1, 640, 128, 1, 1),
    (1, 768, 128, 1, 2),
    (0, 0, 256, 2, 0),
    (0, 256, 384, 2, 1),
    (0, 640, 256, 2, 2),
    (0, 896, 384, 3, 0),
    (0, 1280, 384, 3, 1),
    (0, 1664, 256, 3, 2),
)
GROUPS = ((1, 0, 512, 0), (1, 512, 384, 1), (0, 0, 896, 0), (0, 896, 1024, 1))
COUNT = len(PIECES)
PAIR = (0, 1, 2, 3)
SMALL = (4, 5)
ATTENTION = PAIR + SMALL
FEED = tuple(range(6, COUNT))


def cube_of(piece):
    return GROUPS[piece[3]][3]


NEAR, FAR = CUBES
BLOCKS = tuple((r, c) for r in range(5) for c in range(r, 5))


def order_of(piece):
    return tuple(CUBES[1 - cube_of(piece)][(piece[4] + step) % 3] for step in range(3))


def place():
    f = lax.axis_index("fsdp")
    c = lax.axis_index("ctx")
    return f // 2, (f % 2) * 2 + c // 8, (c // 2) % 4, c % 2


def gray(v):
    return v // 2, (v % 2 + v // 2) % 2


def place_bits(x, z, y, core):
    return gray(x) + gray(z) + gray(y) + (core,)


def partner(where, bits):
    x, z, y, core = where
    for bit in bits:
        if bit == 0:
            x = 3 - x
        elif bit == 1:
            x = x + 1 - 2 * (x % 2)
        elif bit == 2:
            z = 3 - z
        elif bit == 3:
            z = z + 1 - 2 * (z % 2)
        elif bit == 4:
            y = 3 - y
        elif bit == 5:
            y = y + 1 - 2 * (y % 2)
        else:
            core = 1 - core
    return (x * 2 + z // 2, (z % 2) * 8 + y * 2 + core)


def greet(peers):
    barrier = pltpu.get_barrier_semaphore()
    for peer in peers:
        pl.semaphore_signal(barrier, inc=1, device_id=peer, device_id_type=MESH)


def greeted(peers):
    pl.semaphore_wait(pltpu.get_barrier_semaphore(), len(peers))


def remote(src, dst, send_sem, recv_sem, peer):
    return pltpu.make_async_remote_copy(
        src_ref=src,
        dst_ref=dst,
        send_sem=send_sem,
        recv_sem=recv_sem,
        device_id=peer,
        device_id_type=MESH,
    )


def dot_nn(a, b):
    return jnp.dot(a, b, preferred_element_type=F32)


def dot_nt(a, b):
    return lax.dot_general(a, b, (((1,), (1,)), ((), ())), preferred_element_type=F32)


def dot_tn(a, b):
    return lax.dot_general(a, b, (((0,), (0,)), ((), ())), preferred_element_type=F32)


def parts_of(value):
    high = value.astype(BF)
    return high, (value - high.astype(F32)).astype(BF)


def dot_exact(rows, pair):
    high, low = parts_of(rows)
    count = rows.shape[0]
    both = dot_nn(jnp.concatenate([high, low], axis=0), pair[0])
    return both[:count] + both[count:] + dot_nn(high, pair[1])


def fresh_of(grad_rows, moment):
    return MOMENTUM * moment + grad_rows


def inverse_rms(values):
    return lax.rsqrt(jnp.mean(values * values, axis=-1, keepdims=True) + NORM_EPS)


GELU_RATE = math.sqrt(2.0 / math.pi)
GELU_CUBE = 0.044715
TOKENS = 512


def block_kernel(*refs):
    x_ref, cot_hbm = refs[0:2]
    wq, wk, wv, wo, wg, wu, wd = refs[2:9]
    gains_ref, select_hbm, lane_mask, turn = refs[9:13]
    moments = refs[13:20]
    out_hbm, input_grad_hbm = refs[20:22]
    sums, ortho = refs[22:24], refs[24]
    weights, core_in, arrive, owns = refs[25:27], refs[27:29], refs[29:31], refs[31:33]
    (
        pair_own,
        small_own,
        x_prev,
        cot,
        select,
        low,
        query_full,
        output_full,
        key_value_full,
        gain_rows,
        query,
        window,
        probs,
        wide,
        window_cot,
        back_in,
        blocks,
        blocks_in,
        blocks_arrive,
        blocks_whole,
        rows_in,
        rows_out,
    ) = refs[33:55]
    (
        load_sems,
        own_sems,
        send_sems,
        recv_sems,
        pass_send,
        pass_recv,
        half_send,
        half_recv,
        sum_send,
        sum_recv,
        direct_send,
        direct_recv,
        last_send,
        last_recv,
        edge_send,
        edge_recv,
        far_send,
        far_recv,
        block_send,
        block_recv,
        whole_send,
        whole_recv,
        whole_pass_send,
        whole_pass_recv,
        back_send,
        back_recv,
    ) = refs[55:]
    feed_buffer, pair_buffer = weights
    out, middle, second_cot = (wide.at[512 * n : 512 * n + 512] for n in range(3))
    where = place()
    mine = place_bits(*where)
    core = mine[CORE]
    peers = [partner(where, (bit,)) for bit in range(7)]
    f, c = lax.axis_index("fsdp"), lax.axis_index("ctx")
    after, before = (f, (c + 1) % 16), (f, (c + 15) % 16)
    masks = [tuple(n for n in range(3) if mask // (4, 2, 1)[n] % 2) for mask in range(1, 8)]
    far_bits = [tuple(FAR[n] for n in chosen) for chosen in masks]
    near_bits = [tuple(NEAR[n] for n in chosen) for chosen in masks]
    far_peers = [partner(where, bits) for bits in far_bits]
    near_peers = [partner(where, bits) for bits in near_bits]
    met = peers + [after, before]
    met += [peer for peer, bits in zip(far_peers, far_bits) if len(bits) > 1]
    met += [peer for peer, bits in zip(near_peers, near_bits) if len(bits) > 1]
    greet(met)

    loads = [
        pltpu.make_async_copy(cot_hbm, cot, load_sems.at[0]),
        pltpu.make_async_copy(select_hbm, select, load_sems.at[1]),
    ]
    for copy in loads:
        copy.start()
    pair_own[0:8] = wq[...]
    pair_own[8:16] = wo[...]
    small_own[...] = jnp.zeros_like(small_own)
    small_own[0:5] = dot_nn(wk[...].astype(BF), turn[...])
    small_own[8:13] = dot_nn(wv[...].astype(BF), turn[...])
    small_own[5:6, 0:5] = gains_ref[0:1]
    small_own[5:6, 128:133] = gains_ref[1:2]
    for n, value in enumerate((wg, wu, wd)):
        owns[0][:, n * D : n * D + D] = value[...].astype(BF)
    owns[1][:, 0:D] = pair_own[...].astype(BF)
    owns[1][:, D:] = small_own[...].astype(BF)
    greeted(met)

    edge = remote(x_ref, x_prev, edge_send.at[0], edge_recv.at[0], after)
    edge.start()

    local = []
    for array in range(2):
        copy = pltpu.make_async_copy(owns[array], weights[array].at[mine], own_sems.at[array])
        copy.start()
        local.append(copy)
    gather_sends, passed = ({n: [] for n in range(COUNT)} for _ in range(2))
    direct_sends = {}
    gather_steps = {}

    def gathered(n, free, other=None):
        array, first, count = PIECES[n][:3]
        index = tuple(
            ALL if bit in free else (1 - mine[bit] if bit == other else mine[bit])
            for bit in range(7)
        )
        return weights[array].at[index + (ALL, pl.ds(first, count))]

    def pass_on(n, slot, part):
        copy = remote(part, part, pass_send.at[n, slot], pass_recv.at[n, slot], peers[CORE])
        copy.start()
        passed[n].append(copy)

    cube_bits = (near_bits, far_bits)
    cube_peers = (near_peers, far_peers)

    def gather_start(group):
        array, first, count, cube = GROUPS[group]
        columns = pl.ds(first, count)
        direct_sends[group] = []
        for k in range(7):
            copy = remote(
                owns[array].at[:, columns],
                weights[array].at[mine + (ALL, columns)],
                direct_send.at[group, k],
                direct_recv.at[group, k],
                cube_peers[cube][k],
            )
            copy.start()
            direct_sends[group].append(copy)

    def gather_step(n, step):
        order, direct = order_of(PIECES[n]), CUBES[cube_of(PIECES[n])]
        if step > 0:
            gather_steps[n].wait_recv()
        elif n % 3 == 0:
            for copy in direct_sends[n // 3]:
                copy.wait_recv()
        if step < 3:
            part = gathered(n, direct + order[:step])
            copy = remote(
                part, part, send_sems.at[n, step], recv_sems.at[n, step], peers[order[step]]
            )
            copy.start()
            gather_sends[n].append(copy)
            gather_steps[n] = copy
        if step == 1:
            pass_on(n, 0, gathered(n, direct + order[:1]))
        elif step > 1:
            pass_on(n, step - 1, gathered(n, direct + order[: step - 1], order[step - 1]))

    def all_passed(numbers):
        for n in numbers:
            for copy in passed[n]:
                copy.wait_recv()

    for group in range(4):
        gather_start(group)
    for copy in local:
        copy.wait()
    for step in range(3):
        for n in range(COUNT):
            gather_step(n, step)
    for n in ATTENTION:
        gather_step(n, 3)
    for copy in loads:
        copy.wait()
    edge.wait()
    all_passed(ATTENTION)

    small = pair_buffer[(ALL,) * 8 + (slice(D, D + HD),)].reshape(DEVICES, 16, HD).astype(F32)
    rows = jnp.concatenate(
        [small[:, 0:8].reshape(1024, HD), small[:, 8:16].reshape(1024, HD)], axis=1
    ).astype(BF)
    key_value_full[...] = dot_nn(select[0:D], rows).astype(BF)
    lanes = lane_mask[0].astype(F32) + lane_mask[1].astype(F32)
    gain_lanes = (dot_nn(select[D:], rows[:, 0:HD]) * lanes).astype(BF)
    half_of = lax.broadcasted_iota(jnp.int32, (8, HD), 1) // 128
    chooser = (half_of == lax.broadcasted_iota(jnp.int32, (8, HD), 0)).astype(F32).astype(BF)
    gain_rows[...] = dot_nt(chooser, gain_lanes)
    attn_gain, feed_gain = gain_rows[0:1], gain_rows[1:2]

    def normalize(i, carry):
        rows = pl.ds(pl.multiple_of(i * 128, 128), 128)
        for source, target in ((x_prev, x_prev), (x_ref, low)):
            value = source[rows].astype(F32)
            target[rows] = (value * inverse_rms(value) * attn_gain).astype(BF)
        return carry

    lax.fori_loop(0, 4, normalize, 0)

    def project(i, carry):
        rows = pl.ds(pl.multiple_of(i * 256, 256), 256)
        own_rows = pl.ds(pl.multiple_of(TOKENS + i * 256, 256), 256)
        window[rows] = dot_nn(x_prev[rows], key_value_full[...]).astype(BF)
        window[own_rows] = dot_nn(low[rows], key_value_full[...]).astype(BF)
        return carry

    lax.fori_loop(0, 2, project, 0)
    def head_rows(head):
        return pl.ds(pl.multiple_of(head * HD, HD), HD)

    def unpack(head, carry):
        both = pair_buffer[(head // 2, head % 2) + (ALL,) * 6 + (slice(0, D),)]
        both = both.reshape(32, 16, D).astype(F32)
        rows = head_rows(head)
        query_full[rows] = both[:, 0:8].reshape(HD, D).astype(BF)
        output_full[rows] = both[:, 8:16].reshape(HD, D).astype(BF)
        query[head] = dot_nt(low[...], query_full[rows]).astype(BF)
        return carry

    lax.fori_loop(0, HQ, unpack, 0)

    absent = jnp.where(c == 0, -1e30, 0.0).astype(F32)
    score_scale = 1.0 / math.sqrt(HD)

    def upper():
        row = lax.broadcasted_iota(jnp.int32, (512, 256), 0) % 256
        return lax.broadcasted_iota(jnp.int32, (512, 256), 1) > row

    def spread(ends, inner):
        above = jnp.where(upper(), ends, 0.0)
        return jnp.concatenate([above, inner, ends - above], axis=1).astype(BF)

    def attend(b):
        def pair_of_heads(hp, carry):
            heads, rows = pl.ds(2 * hp, 2), slice(256 * b, 256 * b + 256)
            keys = window[256 * b : 256 * b + 768, 0:HD]
            values = window[256 * b : 256 * b + 768, HD:]
            scores = dot_nt(query[heads, rows].reshape(512, HD), keys) * score_scale
            ends = jnp.where(upper(), scores[:, 0:256] + absent, scores[:, 512:])
            inner = scores[:, 256:512]
            if b == 0:
                inner = inner + absent
            top = jnp.maximum(
                jnp.max(ends, axis=-1, keepdims=True), jnp.max(inner, axis=-1, keepdims=True)
            )
            ends, inner = jnp.exp(ends - top), jnp.exp(inner - top)
            total = jnp.sum(ends, axis=-1, keepdims=True) + jnp.sum(inner, axis=-1, keepdims=True)
            ends, inner = ends * (1.0 / total), inner * (1.0 / total)
            probs[2 * b + hp, :, 0:256] = ends
            probs[2 * b + hp, :, 256:] = inner
            mixed = dot_nn(spread(ends, inner), values).astype(BF)
            columns = pl.ds(pl.multiple_of(hp * 512, 512), 512)
            select[rows, columns] = jnp.concatenate([mixed[:256], mixed[256:]], axis=1)
            return carry

        lax.fori_loop(0, 2, pair_of_heads, 0)

    attend(0)
    attend(1)
    for n in FEED:
        gather_step(n, 3)
    def all_sent(numbers):
        for n in numbers:
            for copy in gather_sends[n] + passed[n]:
                copy.wait_send()
            if n % 3 == 0:
                for copy in direct_sends[n // 3]:
                    copy.wait_send()

    all_sent(ATTENTION)

    def second_norm(i, carry):
        rows = pl.ds(pl.multiple_of(i * 256, 256), 256)
        value = x_ref[rows].astype(F32) + dot_nn(select[rows], output_full[...])
        middle[rows] = value
        out[rows] = value
        second_cot[rows] = jnp.zeros((256, D), F32)
        normed = (value * inverse_rms(value) * feed_gain).astype(BF)
        pair_buffer[(0, 0, i) + (ALL,) * 5 + (slice(0, D),)] = normed.reshape((2,) * 4 + (16, D))
        return carry

    lax.fori_loop(0, 2, second_norm, 0)
    all_passed(FEED)
    all_sent(FEED)

    sum_sends, sum_steps, sum_directs = [], {}, {}

    def halve(number):
        if isinstance(number, int) and number >= 4:
            array, lead = 1, (ALL,) * 6
            columns = pl.ds(0, D) if number == 4 else pl.ds(D, HD)
        else:
            array, lead, columns = 0, (number // 2, number % 2) + (ALL,) * 4, ALL
        return remote(
            weights[array].at[lead + (1 - core, ALL, columns)],
            core_in[array].at[lead + (ALL, columns)],
            half_send.at[number],
            half_recv.at[number],
            peers[CORE],
        )

    def sum_send_step(n, step):
        array, first, count = PIECES[n][:3]
        order = order_of(PIECES[n])
        bit = order[step]
        source = tuple(
            mine[b] if b in order[:step] else (1 - mine[b] if b == bit else ALL) for b in range(6)
        )
        target = tuple(mine[b] if b in order[: step + 1] else ALL for b in range(6))
        tail = (ALL, pl.ds(first, count))
        copy = remote(
            weights[array].at[source + (core,) + tail],
            arrive[array].at[target + tail],
            sum_send.at[n, step],
            sum_recv.at[n, step],
            peers[bit],
        )
        copy.start()
        sum_sends.append(copy)
        sum_steps[n] = copy

    def add(into, other, free):
        turns = max(free - 3, 0)

        def some(i, carry):
            lead = tuple(i // 2 ** (turns - 1 - n) % 2 for n in range(turns))
            for index in itertools.product((0, 1), repeat=free - turns):
                into[lead + index] = into[lead + index] + other[lead + index]
            return carry

        if turns > 0:
            lax.fori_loop(0, 2**turns, some, 0)
        else:
            some(0, 0)

    def first_sums(numbers, halves):
        for number in halves:
            half_copies[number].wait_recv()
        for n in numbers:
            array, first, count = PIECES[n][:3]
            tail = (ALL, pl.ds(first, count))
            add(
                weights[array].at[(ALL,) * 6 + (core,) + tail],
                core_in[array].at[(ALL,) * 6 + tail],
                6,
            )
            sum_send_step(n, 0)

    def next_sums(numbers, step):
        for n in numbers:
            array, first, count = PIECES[n][:3]
            order = order_of(PIECES[n])
            bit = order[step]
            tail = (ALL, pl.ds(first, count))
            sum_steps[n].wait_recv()
            here = tuple(mine[b] if b in order[: step + 1] else ALL for b in range(6))
            there = tuple(1 - mine[b] if b == bit else v for b, v in enumerate(here))
            into, other = weights[array].at[here + (core,) + tail], arrive[array].at[there + tail]
            add(into, other, 5 - step)
            if step < 2:
                sum_send_step(n, step + 1)

    def flipped(bits):
        return tuple(1 - mine[b] if b in bits else mine[b] for b in range(6))

    def sum_direct(group):
        array, first, count, cube = GROUPS[group]
        tail = (ALL, pl.ds(first, count))
        sum_directs[group] = []
        for k, bits in enumerate(cube_bits[cube]):
            copy = remote(
                weights[array].at[flipped(bits) + (core,) + tail],
                arrive[array].at[mine[:6] + tail],
                last_send.at[group, k],
                last_recv.at[group, k],
                cube_peers[cube][k],
            )
            copy.start()
            sum_sends.append(copy)
            sum_directs[group].append(copy)

    def last_sums(group):
        array, first, count, cube = GROUPS[group]
        tail = (ALL, pl.ds(first, count))
        total = weights[array][mine[:6] + (core,) + tail].astype(F32)
        for k, bits in enumerate(cube_bits[cube]):
            sum_directs[group][k].wait_recv()
            total = total + arrive[array][flipped(bits) + tail].astype(F32)
        sums[array][:, pl.ds(first, count)] = total

    def feed(j, carry):
        gate_at, up_at, down_at = (
            (j // 2, j % 2) + (ALL,) * 6 + (slice(n * D, n * D + D),) for n in range(3)
        )
        gate_rows = feed_buffer[gate_at].reshape(512, D)
        up_rows = feed_buffer[up_at].reshape(512, D)
        down_rows = feed_buffer[down_at].reshape(512, D)
        second_low = pair_buffer[(0, 0) + (ALL,) * 6 + (slice(0, D),)].reshape(TOKENS, D)
        hidden, gate_cot, up_cot = [], [], []
        for part in range(2):
            tokens = slice(256 * part, 256 * part + 256)
            gate = dot_nt(second_low[tokens], gate_rows)
            up = dot_nt(second_low[tokens], up_rows)
            hidden_cot = dot_nt(cot[tokens], down_rows)
            square = gate * gate
            bend = jnp.tanh(GELU_RATE * gate * (1.0 + GELU_CUBE * square))
            half = 0.5 * (1.0 + bend)
            gelu = gate * half
            slope = half + 0.5 * gate * (1.0 - bend * bend) * (
                GELU_RATE * (1.0 + 3.0 * GELU_CUBE * square)
            )
            hidden.append((gelu * up).astype(BF))
            gate_cot.append((hidden_cot * up * slope).astype(BF))
            up_cot.append((hidden_cot * gelu).astype(BF))
            out[tokens] += dot_nn(hidden[part], down_rows)
            second_cot[tokens] += dot_nn(gate_cot[part], gate_rows) + dot_nn(up_cot[part], up_rows)
        hidden, gate_cot, up_cot = (
            jnp.concatenate(parts, axis=0) for parts in (hidden, gate_cot, up_cot)
        )
        shape = (2,) * 5 + (16, D)
        feed_buffer[down_at] = dot_tn(hidden, cot[...]).astype(BF).reshape(shape)
        feed_buffer[gate_at] = dot_tn(gate_cot, second_low).astype(BF).reshape(shape)
        feed_buffer[up_at] = dot_tn(up_cot, second_low).astype(BF).reshape(shape)
        halve(j).start()
        return carry

    lax.fori_loop(0, 4, feed, 0)
    half_copies = [halve(number) for number in range(6)]

    stores = [pltpu.make_async_copy(out, out_hbm, load_sems.at[2])]
    stores[0].start()

    def second_back(i, total):
        rows = pl.ds(pl.multiple_of(i * 128, 128), 128)
        value = middle[rows]
        rms = inverse_rms(value)
        direct = second_cot[rows]
        total = total + jnp.sum(direct * value * rms, axis=0, keepdims=True)
        scaled = direct * feed_gain
        inner = jnp.mean(value * scaled, axis=-1, keepdims=True)
        value = cot[rows].astype(F32) + rms * scaled - value * (rms * rms * rms * inner)
        middle[rows] = value
        x_prev[rows] = value.astype(BF)
        return total

    feed_gain_cot = lax.fori_loop(0, 4, second_back, jnp.zeros((1, D), F32))

    def output_back(head, carry):
        rows = head_rows(head)
        select[TOKENS : 2 * TOKENS, rows] = dot_nt(x_prev[...], output_full[rows]).astype(BF)
        output_full[rows] = dot_tn(select[0:TOKENS, rows], x_prev[...]).astype(BF)
        return carry

    lax.fori_loop(0, HQ, output_back, 0)
    window_cot[...] = jnp.zeros_like(window_cot)

    def attend_back(b):
        def pair_of_heads(hp, carry):
            heads, rows = pl.ds(2 * hp, 2), slice(256 * b, 256 * b + 256)
            span = slice(256 * b, 256 * b + 768)
            keys, values = window[span, 0:HD], window[span, HD:]
            columns = pl.ds(pl.multiple_of(hp * 512, 512), 512)
            below = slice(TOKENS + 256 * b, TOKENS + 256 * b + 256)
            given = select[below, columns]
            given = jnp.concatenate([given[:, :HD], given[:, HD:]], axis=0)
            ends, inner = probs[2 * b + hp, :, 0:256], probs[2 * b + hp, :, 256:]
            prob_cot = dot_nt(given, values)
            ends_cot = jnp.where(upper(), prob_cot[:, 0:256], prob_cot[:, 512:])
            inner_cot = prob_cot[:, 256:512]
            total = jnp.sum(ends_cot * ends, axis=-1, keepdims=True) + jnp.sum(
                inner_cot * inner, axis=-1, keepdims=True
            )
            score_low = spread(ends * (ends_cot - total), inner * (inner_cot - total))
            query_cot = (dot_nn(score_low, keys) * score_scale).astype(BF)
            select[below, columns] = jnp.concatenate([query_cot[:256], query_cot[256:]], axis=1)
            window_cot[span, 0:HD] += dot_tn(score_low, query[heads, rows].reshape(512, HD))
            window_cot[span, HD:] += dot_tn(spread(ends, inner), given)
            return carry

        lax.fori_loop(0, 2, pair_of_heads, 0)

    def send_back(half):
        rows = slice(256 * half, 256 * half + 256)
        window[rows, 0:HD] = (window_cot[rows, 0:HD] * score_scale).astype(BF)
        window[rows, HD:] = window_cot[rows, HD:].astype(BF)
        copy = remote(
            window.at[rows], back_in.at[rows], edge_send.at[1 + half], edge_recv.at[1 + half], before
        )
        copy.start()
        return copy

    attend_back(0)
    backs = [send_back(0)]
    first_sums(FEED, range(4))
    attend_back(1)
    backs.append(send_back(1))

    def query_back(head, carry):
        rows = head_rows(head)
        both = jnp.concatenate(
            [
                dot_tn(select[TOKENS : 2 * TOKENS, rows], low[...]).reshape(32, 8, D),
                output_full[rows].astype(F32).reshape(32, 8, D),
            ],
            axis=1,
        )
        pair_buffer[(head // 2, head % 2) + (ALL,) * 6 + (slice(0, D),)] = (
            both.astype(BF).reshape((2,) * 5 + (16, D))
        )
        return carry

    lax.fori_loop(0, HQ, query_back, 0)
    half_copies[4].start()

    def first_back(i, carry):
        rows = pl.ds(pl.multiple_of(i * 256, 256), 256)
        below = pl.ds(pl.multiple_of(TOKENS + i * 256, 256), 256)
        second_cot[rows] = dot_nn(select[below], query_full[...])
        return carry

    lax.fori_loop(0, 2, first_back, 0)
    again = pltpu.make_async_copy(select_hbm, select, load_sems.at[1])
    again.start()
    first_sums(PAIR, (4,))
    for copy in backs:
        copy.wait()
    returned = back_in[...].astype(F32)
    edge_low = jnp.concatenate(
        [
            window_cot[TOKENS:, 0:HD] * score_scale + returned[:, 0:HD],
            window_cot[TOKENS:, HD:] + returned[:, HD:],
        ],
        axis=1,
    ).astype(BF)
    window[TOKENS:] = edge_low
    key_value_grad = dot_tn(low[...], edge_low).astype(BF)

    def first_gain(i, total):
        rows = pl.ds(pl.multiple_of(i * 256, 256), 256)
        own_rows = pl.ds(pl.multiple_of(TOKENS + i * 256, 256), 256)
        direct = second_cot[rows] + dot_nt(window[own_rows], key_value_full[...])
        second_cot[rows] = direct
        value = x_ref[rows].astype(F32)
        return total + jnp.sum(direct * value * inverse_rms(value), axis=0, keepdims=True)

    attn_gain_cot = lax.fori_loop(0, 2, first_gain, jnp.zeros((1, D), F32))

    def as_columns(row):
        return dot_tn(jnp.broadcast_to(row, (8, D)), jnp.full((8, HD), 0.125, F32))

    gain_cots = as_columns(attn_gain_cot) * lane_mask[0].astype(F32) + as_columns(
        feed_gain_cot
    ) * lane_mask[1].astype(F32)
    again.wait()
    key_value_rows = dot_tn(select[0:D], key_value_grad)
    gain_cot_rows = dot_tn(select[D:], gain_cots.astype(BF))
    both = jnp.concatenate(
        [
            (key_value_rows[:, 0:HD] + gain_cot_rows).reshape(DEVICES, 8, HD),
            key_value_rows[:, HD:].reshape(DEVICES, 8, HD),
        ],
        axis=1,
    )
    pair_buffer[(ALL,) * 8 + (slice(D, D + HD),)] = both.astype(BF).reshape((2,) * 7 + (16, HD))
    half_copies[5].start()
    next_sums(FEED, 0)
    next_sums(PAIR, 0)

    def input_back(i, carry):
        rows = pl.ds(pl.multiple_of(i * 128, 128), 128)
        value = x_ref[rows].astype(F32)
        rms = inverse_rms(value)
        scaled = second_cot[rows] * attn_gain
        inner = jnp.mean(value * scaled, axis=-1, keepdims=True)
        second_cot[rows] = middle[rows] + rms * scaled - value * (rms * rms * rms * inner)
        return carry

    first_sums(SMALL, (5,))
    lax.fori_loop(0, 4, input_back, 0)
    stores.append(pltpu.make_async_copy(second_cot, input_grad_hbm, load_sems.at[3]))
    stores[1].start()
    next_sums(FEED, 1)
    next_sums(PAIR, 1)
    next_sums(SMALL, 0)
    next_sums(FEED, 2)
    sum_direct(2)
    sum_direct(3)
    next_sums(PAIR, 2)
    sum_direct(0)
    next_sums(SMALL, 1)
    next_sums(SMALL, 2)
    sum_direct(1)
    last_sums(2)
    last_sums(3)
    last_sums(0)
    last_sums(1)
    small = sums[1][:, D:]
    natural = lax.dot_general(
        small,
        turn[...].astype(F32),
        (((1,), (1,)), ((), ())),
        precision=lax.Precision.HIGHEST,
        preferred_element_type=F32,
    )
    gain_row = lax.broadcasted_iota(jnp.int32, (16, HD), 0) == 5
    sums[1][:, D:] = jnp.where(gain_row, small, natural)
    for copy in stores:
        copy.wait()

    now, outgo, result = wide.at[0:D], wide.at[D : D + 128], wide.at[D + 128 : D + 256]
    outgo[...] = jnp.zeros((128, D), F32)
    for n in range(3):
        outgo[16 * n : 16 * n + 16] = fresh_of(sums[0][:, n * D : n * D + D], moments[4 + n][...])
    outgo[48:56] = fresh_of(sums[1][0:8, 0:D], moments[0][...])
    outgo[72:80] = fresh_of(sums[1][8:16, 0:D], moments[3][...])
    outgo[80:85, 0:HD] = fresh_of(sums[1][0:5, D:], moments[1][...])
    outgo[96:101, 0:HD] = fresh_of(sums[1][8:13, D:], moments[2][...])
    rows_out[...] = outgo[...].astype(BF)
    group = mine[0] * 4 + mine[2] * 2 + mine[4]

    def far_group(bits):
        flipped = [1 - mine[bit] if bit in bits else mine[bit] for bit in FAR]
        return flipped[0] * 4 + flipped[1] * 2 + flipped[2]

    def sixteen(ref, number):
        return ref.at[pl.ds(pl.multiple_of(number * 16, 16), 16)]

    copies = []
    for n, bits in enumerate(far_bits):
        copy = remote(
            sixteen(rows_out, far_group(bits)),
            sixteen(rows_in, group),
            far_send.at[n],
            far_recv.at[n],
            far_peers[n],
        )
        copy.start()
        copies.append(copy)
    sixteen(rows_in, group)[...] = sixteen(rows_out, group)[...]
    for copy in copies:
        copy.wait_recv()
    rows = rows_in[...]

    def block_at(number):
        return (number // 8, number // 4 % 2, number // 2 % 2, number % 2)

    for r in range(5):
        strip = dot_tn(rows[:, 128 * r : 128 * r + 128], rows[:, 128 * r :])
        for number, (row, column) in enumerate(BLOCKS):
            if row == r:
                at = 128 * (column - r)
                blocks[block_at(number)] = strip[:, at : at + 128]
    blocks[block_at(15)] = jnp.zeros((128, 128), F32)
    near_mine = tuple(mine[bit] for bit in NEAR)

    def near_of(bits):
        return tuple(1 - mine[bit] if bit in bits else mine[bit] for bit in NEAR)

    halves = remote(
        blocks.at[1 - core], blocks_in, block_send.at[7], block_recv.at[7], peers[CORE]
    )
    halves.start()
    halves.wait()
    blocks[core] = blocks[core] + blocks_in[...]
    block_copies = []
    for n, bits in enumerate(near_bits):
        copy = remote(
            blocks.at[(core,) + near_of(bits)],
            blocks_arrive.at[near_mine],
            block_send.at[n],
            block_recv.at[n],
            near_peers[n],
        )
        copy.start()
        block_copies.append(copy)
    total = blocks[(core,) + near_mine]
    for copy in block_copies:
        copy.wait_recv()
    for n, bits in enumerate(near_bits):
        total = total + blocks_arrive[near_of(bits)]
    own_block = blocks_whole.at[(core,) + near_mine]
    own_block[...] = total
    whole_copies, whole_passed = [], []

    def whole_pass(n, part):
        copy = remote(
            part, part, whole_pass_send.at[n], whole_pass_recv.at[n], peers[CORE]
        )
        copy.start()
        whole_passed.append(copy)

    for n, bits in enumerate(near_bits):
        copy = remote(own_block, own_block, whole_send.at[n], whole_recv.at[n], near_peers[n])
        copy.start()
        whole_copies.append(copy)
    whole_pass(7, own_block)
    for n, bits in enumerate(near_bits):
        whole_copies[n].wait_recv()
        whole_pass(n, blocks_whole.at[(core,) + near_of(bits)])
    for copy in whole_passed:
        copy.wait_recv()
    square_sum = jnp.zeros((1, 1), F32)
    same = lax.broadcasted_iota(jnp.int32, (128, 128), 0) == lax.broadcasted_iota(
        jnp.int32, (128, 128), 1
    )
    for number, (row, column) in enumerate(BLOCKS):
        if row == column:
            diagonal = jnp.where(same, blocks_whole[block_at(number)], 0.0)
            square_sum = square_sum + jnp.sum(
                jnp.sum(diagonal, axis=0, keepdims=True), axis=1, keepdims=True
            )
    factor = 1.0 / (jnp.sqrt(square_sum) + ORTHO_EPS)
    for number, (row, column) in enumerate(BLOCKS):
        part = blocks_whole[block_at(number)] * (factor * factor)
        now[128 * row : 128 * row + 128, 128 * column : 128 * column + 128] = part
        if row != column:
            now[128 * column : 128 * column + 128, 128 * row : 128 * row + 128] = part.T
    result[...] = rows_in[...].astype(F32) * factor
    gram_high, gram_low = select.at[0:D, 0:D], select.at[D : 2 * D, 0:D]
    poly_high, poly_low = query_full.at[0:D], output_full.at[0:D]
    gram_high[...] = now[...].astype(BF)

    def iterate(_, carry):
        change = POLY_SECOND * now[...] + POLY_THIRD * dot_nn(gram_high[...], gram_high[...])
        poly_high[...] = change.astype(BF)
        result[...] = POLY_FIRST * result[...] + dot_nn(result[...].astype(BF), poly_high[...])
        product = POLY_FIRST * now[...] + dot_nn(gram_high[...], poly_high[...])
        gram_low[...] = product.astype(BF)
        later = POLY_FIRST * product + dot_nn(gram_low[...], poly_high[...])
        now[...] = later
        gram_high[...] = later.astype(BF)
        return carry

    lax.fori_loop(0, NS_ITERS - 2, iterate, 0)
    gram_value = now[...]
    change = POLY_SECOND * gram_value + POLY_THIRD * dot_nn(gram_high[...], gram_high[...])
    poly_high[...], poly_low[...] = parts_of(change)
    gram_low[...] = (gram_value - gram_high[...].astype(F32)).astype(BF)
    gram, poly = (gram_high[...], gram_low[...]), (poly_high[...], poly_low[...])
    value = POLY_FIRST * result[...] + dot_exact(result[...], poly)

    def times_next_gram(rows):
        rows = dot_exact(rows, gram)
        rows = POLY_FIRST * rows + dot_exact(rows, poly)
        return POLY_FIRST * rows + dot_exact(rows, poly)

    once = times_next_gram(value)
    for copy in copies:
        copy.wait_send()
    rows_out[...] = (
        POLY_FIRST * value + POLY_SECOND * once + POLY_THIRD * times_next_gram(once)
    ).astype(BF)
    copies = []
    for n, bits in enumerate(far_bits):
        copy = remote(
            sixteen(rows_out, far_group(bits)),
            ortho.at[group],
            back_send.at[n],
            back_recv.at[n],
            far_peers[n],
        )
        copy.start()
        copies.append(copy)
    ortho[group] = sixteen(rows_out, group)[...]
    for copy in copies:
        copy.wait()
    for copy in block_copies + whole_copies + whole_passed:
        copy.wait_send()
    for copy in half_copies:
        copy.wait_send()
    for copy in sum_sends:
        copy.wait_send()


def block_constants():
    swap = np.array([0, 1, 3, 2])
    position = np.arange(DEVICES).reshape(4, 4, 4, 2)[swap][:, swap][:, :, swap].reshape(DEVICES)
    select = np.zeros((2 * D, 8 * DEVICES), np.float32)
    lane_mask = np.zeros((2, D, HD), np.float32)
    for i in range(D):
        select[i, position[i // 5] * 8 + i % 5] = 1.0
        select[D + i, position[i // 5] * 8 + 5] = 1.0
        lane_mask[0, i, i % 5] = 1.0
        lane_mask[1, i, 128 + i % 5] = 1.0
    index = np.arange(HD).reshape(4, 4, 16)[swap][:, swap].reshape(HD)
    turn = np.eye(HD, dtype=np.float32)[:, index]
    return tuple(jnp.asarray(part, BF) for part in (select, lane_mask, turn))


def block(inputs, cotangent, masters, norm_gains, moments):
    select, lane_mask, turn = block_constants()
    vmem = pl.BlockSpec(memory_space=pltpu.VMEM)
    anywhere = pl.BlockSpec(memory_space=pl.ANY)
    dma = pltpu.SemaphoreType.DMA
    halves = [pltpu.VMEM((2,) * 6 + (16, width), BF) for width in WIDTHS]
    results = pl.pallas_call(
        block_kernel,
        out_shape=[jax.ShapeDtypeStruct((TOKENS, D), F32)] * 2
        + [jax.ShapeDtypeStruct((16, width), F32) for width in WIDTHS]
        + [jax.ShapeDtypeStruct((8, 16, D), BF)],
        in_specs=[vmem, anywhere] + [vmem] * 8 + [anywhere, vmem, vmem] + [vmem] * 7,
        out_specs=[anywhere] * 2 + [vmem] * 3,
        scratch_shapes=[pltpu.VMEM((2,) * 7 + (16, width), BF) for width in WIDTHS]
        + halves
        + halves
        + [pltpu.VMEM((16, width), BF) for width in WIDTHS]
        + [
            pltpu.VMEM((16, D), F32),
            pltpu.VMEM((16, HD), F32),
            pltpu.VMEM((TOKENS, D), BF),
            pltpu.VMEM((TOKENS, D), BF),
            pltpu.VMEM((2 * D, 8 * DEVICES), BF),
            pltpu.VMEM((TOKENS, D), BF),
            pltpu.VMEM((HQ * HD, D), BF),
            pltpu.VMEM((HQ * HD, D), BF),
            pltpu.VMEM((D, 2 * HD), BF),
            pltpu.VMEM((8, D), F32),
            pltpu.VMEM((HQ, TOKENS, HD), BF),
            pltpu.VMEM((2 * TOKENS, 2 * HD), BF),
            pltpu.VMEM((4, 512, 512), F32),
            pltpu.VMEM((3 * TOKENS, D), F32),
            pltpu.VMEM((2 * TOKENS, 2 * HD), F32),
            pltpu.VMEM((TOKENS, 2 * HD), BF),
            pltpu.VMEM((2, 2, 2, 2, 128, 128), F32),
            pltpu.VMEM((2, 2, 2, 128, 128), F32),
            pltpu.VMEM((2, 2, 2, 128, 128), F32),
            pltpu.VMEM((2, 2, 2, 2, 128, 128), F32),
            pltpu.VMEM((128, D), BF),
            pltpu.VMEM((128, D), BF),
            dma((4,)),
            dma((2,)),
            dma((COUNT, 3)),
            dma((COUNT, 3)),
            dma((COUNT, 3)),
            dma((COUNT, 3)),
            dma((6,)),
            dma((6,)),
            dma((COUNT, 3)),
            dma((COUNT, 3)),
            dma((4, 7)),
            dma((4, 7)),
            dma((4, 7)),
            dma((4, 7)),
            dma((3,)),
            dma((3,)),
            dma((7,)),
            dma((7,)),
            dma((8,)),
            dma((8,)),
            dma((7,)),
            dma((7,)),
            dma((8,)),
            dma((8,)),
            dma((7,)),
            dma((7,)),
        ],
        compiler_params=pltpu.CompilerParams(
            collective_id=0, has_side_effects=True, vmem_limit_bytes=59 * 2**20
        ),
        name="block",
    )(inputs, cotangent, *masters, norm_gains, select, lane_mask, turn, *moments)
    return results[0:2], results[2:4], results[4]


SIZES = ((D, HQ * HD), (D, HD), (D, HD), (HQ * HD, D), (D, FF), (D, FF), (FF, D))


def finish_kernel(*refs):
    feed, rest, ortho = refs[:3]
    moments, masters, gains, large = refs[3:10], refs[10:17], refs[17:20], refs[20:22]
    grad_outs, moment_outs, master_outs, gain_outs, large_outs = (
        refs[22:29],
        refs[29:36],
        refs[36:43],
        refs[43:47],
        refs[47:49],
    )
    held, sems = refs[49:51]
    copies = [
        pltpu.make_async_copy(large[n], held.at[n], sems.at[n]) for n in range(2)
    ]
    for copy in copies:
        copy.start()
    stores = []
    for n in range(2):
        copies[n].wait()
        stores.append(pltpu.make_async_copy(held.at[n], large_outs[n], sems.at[2 + n]))
        stores[n].start()
    own = (
        rest[0:8, 0:D],
        rest[0:5, D:],
        rest[8:13, D:],
        rest[8:16, 0:D],
        feed[:, 0:D],
        feed[:, D : 2 * D],
        feed[:, 2 * D :],
    )
    turned = tuple(ortho[n].astype(F32) for n in range(7))
    turned = (
        turned[3][0:8],
        turned[5][0:5, 0:HD],
        turned[6][0:5, 0:HD],
        turned[4][8:16],
        turned[0],
        turned[1],
        turned[2],
    )
    for n in range(7):
        rows, columns = SIZES[n]
        ratio = math.sqrt(max(rows, columns) / rows)
        grad_outs[n][...] = own[n]
        moment_outs[n][...] = fresh_of(own[n], moments[n][...])
        master_outs[n][...] = (
            masters[n][...] * (1.0 - MUON_RATE * MUON_DECAY) - MUON_RATE * ratio * turned[n]
        )
    gain_grads = jnp.concatenate([rest[5:6, D : D + 5], rest[5:6, D + 128 : D + 133]], axis=0)
    norm_gains, gain_first, gain_second = (ref[...] for ref in gains)
    first_moments = BETA_FIRST * gain_first + (1.0 - BETA_FIRST) * gain_grads
    second_moments = BETA_SECOND * gain_second + (1.0 - BETA_SECOND) * gain_grads * gain_grads
    first_hat = first_moments / (1.0 - BETA_FIRST**ADAM_STEP)
    second_hat = second_moments / (1.0 - BETA_SECOND**ADAM_STEP)
    gain_outs[0][...] = gain_grads
    gain_outs[1][...] = first_moments
    gain_outs[2][...] = second_moments
    gain_outs[3][...] = norm_gains - ADAM_RATE * first_hat / (jnp.sqrt(second_hat) + ADAM_EPS)
    for copy in stores:
        copy.wait()


def finish(grads, ortho, moments, masters, gains, large):
    shapes = [jax.ShapeDtypeStruct(moment.shape, F32) for moment in moments]
    vmem = pl.BlockSpec(memory_space=pltpu.VMEM)
    anywhere = pl.BlockSpec(memory_space=pl.ANY)
    return pl.pallas_call(
        finish_kernel,
        out_shape=shapes * 3
        + [jax.ShapeDtypeStruct((2, 5), F32)] * 4
        + [jax.ShapeDtypeStruct((TOKENS, D), F32)] * 2,
        in_specs=[vmem] * 20 + [anywhere] * 2,
        out_specs=[vmem] * 25 + [anywhere] * 2,
        scratch_shapes=[pltpu.VMEM((2, TOKENS, D), F32), pltpu.SemaphoreType.DMA((4,))],
        name="finish",
    )(*grads, ortho, *moments, *masters, *gains, *large)


def body(
    inputs,
    cotangent,
    query_weight,
    key_weight,
    value_weight,
    output_weight,
    gate_weight,
    up_weight,
    down_weight,
    norm_gains,
    query_moment,
    key_moment,
    value_moment,
    output_moment,
    gate_moment,
    up_moment,
    down_moment,
    gain_first,
    gain_second,
):
    moments = (
        query_moment.T,
        key_moment,
        value_moment,
        output_moment,
        gate_moment.T,
        up_moment.T,
        down_moment,
    )
    masters = (
        query_weight.T,
        key_weight,
        value_weight,
        output_weight,
        gate_weight.T,
        up_weight.T,
        down_weight,
    )
    large, grads, ortho = block(inputs, cotangent, masters, norm_gains, moments)
    outs = finish(grads, ortho, moments, masters, (norm_gains, gain_first, gain_second), large)

    def natural(seven):
        return tuple(part.T if n in (0, 4, 5) else part for n, part in enumerate(seven))

    return (
        tuple(outs[25:27])
        + natural(outs[0:7])
        + natural(outs[7:14])
        + natural(outs[14:21])
        + tuple(outs[21:25])
    )


def solution(mesh):
    rows, columns = P(AXES, None), P(None, AXES)
    seven = (columns, rows, rows, rows, columns, columns, rows)
    return jax.shard_map(
        body,
        mesh=mesh,
        in_specs=(rows, rows) + seven + (columns,) + seven + (columns, columns),
        out_specs=(rows, rows) + seven * 3 + (columns,) * 4,
        check_vma=False,
    )
```

```python
import itertools
import math

import jax
import jax.numpy as jnp
import numpy as np
from jax import lax
from jax.experimental import pallas as pl
from jax.experimental.pallas import tpu as pltpu
from jax.sharding import PartitionSpec as P

HQ = 4
HD = 256
D = 640
FF = 2048
WINDOW = 512
NS_ITERS = 4
ADAM_STEP = 10
DEVICES = 128

NORM_EPS = 1e-06
ORTHO_EPS = 1e-07
POLY_FIRST = 3.4445
POLY_SECOND = -4.775
POLY_THIRD = 2.0315
MOMENTUM = 0.95
MUON_RATE = 0.6
MUON_DECAY = 0.01
ADAM_RATE = 0.7
BETA_FIRST = 0.9
BETA_SECOND = 0.999
ADAM_EPS = 1e-08

AXES = ("fsdp", "ctx")
MESH = pl.DeviceIdType.MESH
ALL = slice(None)
BF = jnp.bfloat16
F32 = jnp.float32

CORE = 6
WIDTHS = (3 * D, D + HD)
CUBES = ((1, 5, 3), (0, 2, 4))
PIECES = (
    (1, 0, 256, 0, 0),
    (1, 256, 128, 0, 1),
    (1, 384, 128, 0, 2),
    (1, 512, 128, 1, 0),
    (1, 640, 128, 1, 1),
    (1, 768, 128, 1, 2),
    (0, 0, 256, 2, 0),
    (0, 256, 384, 2, 1),
    (0, 640, 256, 2, 2),
    (0, 896, 384, 3, 0),
    (0, 1280, 384, 3, 1),
    (0, 1664, 256, 3, 2),
)
GROUPS = ((1, 0, 512, 0), (1, 512, 384, 1), (0, 0, 896, 0), (0, 896, 1024, 1))
COUNT = len(PIECES)
PAIR = (0, 1, 2, 3)
SMALL = (4, 5)
ATTENTION = PAIR + SMALL
FEED = tuple(range(6, COUNT))


def cube_of(piece):
    return GROUPS[piece[3]][3]


NEAR, FAR = CUBES
BLOCKS = tuple((r, c) for r in range(5) for c in range(r, 5))


def order_of(piece):
    return tuple(CUBES[1 - cube_of(piece)][(piece[4] + step) % 3] for step in range(3))


def place():
    f = lax.axis_index("fsdp")
    c = lax.axis_index("ctx")
    return f // 2, (f % 2) * 2 + c // 8, (c // 2) % 4, c % 2


def gray(v):
    return v // 2, (v % 2 + v // 2) % 2


def place_bits(x, z, y, core):
    return gray(x) + gray(z) + gray(y) + (core,)


def partner(where, bits):
    x, z, y, core = where
    for bit in bits:
        if bit == 0:
            x = 3 - x
        elif bit == 1:
            x = x + 1 - 2 * (x % 2)
        elif bit == 2:
            z = 3 - z
        elif bit == 3:
            z = z + 1 - 2 * (z % 2)
        elif bit == 4:
            y = 3 - y
        elif bit == 5:
            y = y + 1 - 2 * (y % 2)
        else:
            core = 1 - core
    return (x * 2 + z // 2, (z % 2) * 8 + y * 2 + core)


def greet(peers):
    barrier = pltpu.get_barrier_semaphore()
    for peer in peers:
        pl.semaphore_signal(barrier, inc=1, device_id=peer, device_id_type=MESH)


def greeted(peers):
    pl.semaphore_wait(pltpu.get_barrier_semaphore(), len(peers))


def remote(src, dst, send_sem, recv_sem, peer):
    return pltpu.make_async_remote_copy(
        src_ref=src,
        dst_ref=dst,
        send_sem=send_sem,
        recv_sem=recv_sem,
        device_id=peer,
        device_id_type=MESH,
    )


def dot_nn(a, b):
    return jnp.dot(a, b, preferred_element_type=F32)


def dot_nt(a, b):
    return lax.dot_general(a, b, (((1,), (1,)), ((), ())), preferred_element_type=F32)


def dot_tn(a, b):
    return lax.dot_general(a, b, (((0,), (0,)), ((), ())), preferred_element_type=F32)


def parts_of(value):
    high = value.astype(BF)
    return high, (value - high.astype(F32)).astype(BF)


def dot_exact(rows, pair):
    high, low = parts_of(rows)
    count = rows.shape[0]
    both = dot_nn(jnp.concatenate([high, low], axis=0), pair[0])
    return both[:count] + both[count:] + dot_nn(high, pair[1])


def fresh_of(grad_rows, moment):
    return MOMENTUM * moment + grad_rows


def inverse_rms(values):
    return lax.rsqrt(jnp.mean(values * values, axis=-1, keepdims=True) + NORM_EPS)


GELU_RATE = math.sqrt(2.0 / math.pi)
GELU_CUBE = 0.044715
TOKENS = 512


def block_kernel(*refs):
    x_ref, cot_hbm = refs[0:2]
    wq, wk, wv, wo, wg, wu, wd = refs[2:9]
    gains_ref, select_hbm, lane_mask, turn = refs[9:13]
    moments = refs[13:20]
    out_hbm, input_grad_hbm = refs[20:22]
    sums, ortho = refs[22:24], refs[24]
    weights, core_in, arrive, owns = refs[25:27], refs[27:29], refs[29:31], refs[31:33]
    (
        pair_own,
        small_own,
        x_prev,
        cot,
        select,
        low,
        query_full,
        output_full,
        key_value_full,
        gain_rows,
        query,
        window,
        probs,
        wide,
        window_cot,
        back_in,
        blocks,
        blocks_in,
        blocks_arrive,
        blocks_whole,
        rows_in,
        rows_out,
    ) = refs[33:55]
    (
        load_sems,
        own_sems,
        send_sems,
        recv_sems,
        pass_send,
        pass_recv,
        half_send,
        half_recv,
        sum_send,
        sum_recv,
        direct_send,
        direct_recv,
        last_send,
        last_recv,
        edge_send,
        edge_recv,
        far_send,
        far_recv,
        block_send,
        block_recv,
        whole_send,
        whole_recv,
        whole_pass_send,
        whole_pass_recv,
        back_send,
        back_recv,
    ) = refs[55:]
    feed_buffer, pair_buffer = weights
    out, middle, second_cot = (wide.at[512 * n : 512 * n + 512] for n in range(3))
    where = place()
    mine = place_bits(*where)
    core = mine[CORE]
    peers = [partner(where, (bit,)) for bit in range(7)]
    f, c = lax.axis_index("fsdp"), lax.axis_index("ctx")
    after, before = (f, (c + 1) % 16), (f, (c + 15) % 16)
    masks = [tuple(n for n in range(3) if mask // (4, 2, 1)[n] % 2) for mask in range(1, 8)]
    far_bits = [tuple(FAR[n] for n in chosen) for chosen in masks]
    near_bits = [tuple(NEAR[n] for n in chosen) for chosen in masks]
    far_peers = [partner(where, bits) for bits in far_bits]
    near_peers = [partner(where, bits) for bits in near_bits]
    met = peers + [after, before]
    met += [peer for peer, bits in zip(far_peers, far_bits) if len(bits) > 1]
    met += [peer for peer, bits in zip(near_peers, near_bits) if len(bits) > 1]
    greet(met)

    loads = [
        pltpu.make_async_copy(cot_hbm, cot, load_sems.at[0]),
        pltpu.make_async_copy(select_hbm, select, load_sems.at[1]),
    ]
    for copy in loads:
        copy.start()
    pair_own[0:8] = wq[...]
    pair_own[8:16] = wo[...]
    small_own[...] = jnp.zeros_like(small_own)
    small_own[0:5] = dot_nn(wk[...].astype(BF), turn[...])
    small_own[8:13] = dot_nn(wv[...].astype(BF), turn[...])
    small_own[5:6, 0:5] = gains_ref[0:1]
    small_own[5:6, 128:133] = gains_ref[1:2]
    for n, value in enumerate((wg, wu, wd)):
        owns[0][:, n * D : n * D + D] = value[...].astype(BF)
    owns[1][:, 0:D] = pair_own[...].astype(BF)
    owns[1][:, D:] = small_own[...].astype(BF)
    greeted(met)

    edge = remote(x_ref, x_prev, edge_send.at[0], edge_recv.at[0], after)
    edge.start()

    local = []
    for array in range(2):
        copy = pltpu.make_async_copy(owns[array], weights[array].at[mine], own_sems.at[array])
        copy.start()
        local.append(copy)
    gather_sends, passed = ({n: [] for n in range(COUNT)} for _ in range(2))
    direct_sends = {}
    gather_steps = {}

    def gathered(n, free, other=None):
        array, first, count = PIECES[n][:3]
        index = tuple(
            ALL if bit in free else (1 - mine[bit] if bit == other else mine[bit])
            for bit in range(7)
        )
        return weights[array].at[index + (ALL, pl.ds(first, count))]

    def pass_on(n, slot, part):
        copy = remote(part, part, pass_send.at[n, slot], pass_recv.at[n, slot], peers[CORE])
        copy.start()
        passed[n].append(copy)

    cube_bits = (near_bits, far_bits)
    cube_peers = (near_peers, far_peers)

    def gather_start(group):
        array, first, count, cube = GROUPS[group]
        columns = pl.ds(first, count)
        direct_sends[group] = []
        for k in range(7):
            copy = remote(
                owns[array].at[:, columns],
                weights[array].at[mine + (ALL, columns)],
                direct_send.at[group, k],
                direct_recv.at[group, k],
                cube_peers[cube][k],
            )
            copy.start()
            direct_sends[group].append(copy)

    def gather_step(n, step):
        order, direct = order_of(PIECES[n]), CUBES[cube_of(PIECES[n])]
        if step > 0:
            gather_steps[n].wait_recv()
        elif n % 3 == 0:
            for copy in direct_sends[n // 3]:
                copy.wait_recv()
        if step < 3:
            part = gathered(n, direct + order[:step])
            copy = remote(
                part, part, send_sems.at[n, step], recv_sems.at[n, step], peers[order[step]]
            )
            copy.start()
            gather_sends[n].append(copy)
            gather_steps[n] = copy
        if step == 1:
            pass_on(n, 0, gathered(n, direct + order[:1]))
        elif step > 1:
            pass_on(n, step - 1, gathered(n, direct + order[: step - 1], order[step - 1]))

    def all_passed(numbers):
        for n in numbers:
            for copy in passed[n]:
                copy.wait_recv()

    for group in range(4):
        gather_start(group)
    for copy in local:
        copy.wait()
    for step in range(3):
        for n in range(COUNT):
            gather_step(n, step)
    for n in ATTENTION:
        gather_step(n, 3)
    for copy in loads:
        copy.wait()
    edge.wait()
    all_passed(ATTENTION)

    small = pair_buffer[(ALL,) * 8 + (slice(D, D + HD),)].reshape(DEVICES, 16, HD).astype(F32)
    rows = jnp.concatenate(
        [small[:, 0:8].reshape(1024, HD), small[:, 8:16].reshape(1024, HD)], axis=1
    ).astype(BF)
    key_value_full[...] = dot_nn(select[0:D], rows).astype(BF)
    lanes = lane_mask[0].astype(F32) + lane_mask[1].astype(F32)
    gain_lanes = (dot_nn(select[D:], rows[:, 0:HD]) * lanes).astype(BF)
    half_of = lax.broadcasted_iota(jnp.int32, (8, HD), 1) // 128
    chooser = (half_of == lax.broadcasted_iota(jnp.int32, (8, HD), 0)).astype(F32).astype(BF)
    gain_rows[...] = dot_nt(chooser, gain_lanes)
    attn_gain, feed_gain = gain_rows[0:1], gain_rows[1:2]

    def normalize(i, carry):
        rows = pl.ds(pl.multiple_of(i * 128, 128), 128)
        for source, target in ((x_prev, x_prev), (x_ref, low)):
            value = source[rows].astype(F32)
            target[rows] = (value * inverse_rms(value) * attn_gain).astype(BF)
        return carry

    lax.fori_loop(0, 4, normalize, 0)

    def project(i, carry):
        rows = pl.ds(pl.multiple_of(i * 256, 256), 256)
        own_rows = pl.ds(pl.multiple_of(TOKENS + i * 256, 256), 256)
        window[rows] = dot_nn(x_prev[rows], key_value_full[...]).astype(BF)
        window[own_rows] = dot_nn(low[rows], key_value_full[...]).astype(BF)
        return carry

    lax.fori_loop(0, 2, project, 0)
    def head_rows(head):
        return pl.ds(pl.multiple_of(head * HD, HD), HD)

    def unpack(head, carry):
        both = pair_buffer[(head // 2, head % 2) + (ALL,) * 6 + (slice(0, D),)]
        both = both.reshape(32, 16, D).astype(F32)
        rows = head_rows(head)
        query_full[rows] = both[:, 0:8].reshape(HD, D).astype(BF)
        output_full[rows] = both[:, 8:16].reshape(HD, D).astype(BF)
        query[head] = dot_nt(low[...], query_full[rows]).astype(BF)
        return carry

    lax.fori_loop(0, HQ, unpack, 0)

    absent = jnp.where(c == 0, -1e30, 0.0).astype(F32)
    score_scale = 1.0 / math.sqrt(HD)

    def upper():
        row = lax.broadcasted_iota(jnp.int32, (512, 256), 0) % 256
        return lax.broadcasted_iota(jnp.int32, (512, 256), 1) > row

    def spread(ends, inner):
        above = jnp.where(upper(), ends, 0.0)
        return jnp.concatenate([above, inner, ends - above], axis=1).astype(BF)

    def attend(b):
        def pair_of_heads(hp, carry):
            heads, rows = pl.ds(2 * hp, 2), slice(256 * b, 256 * b + 256)
            keys = window[256 * b : 256 * b + 768, 0:HD]
            values = window[256 * b : 256 * b + 768, HD:]
            scores = dot_nt(query[heads, rows].reshape(512, HD), keys) * score_scale
            ends = jnp.where(upper(), scores[:, 0:256] + absent, scores[:, 512:])
            inner = scores[:, 256:512]
            if b == 0:
                inner = inner + absent
            top = jnp.maximum(
                jnp.max(ends, axis=-1, keepdims=True), jnp.max(inner, axis=-1, keepdims=True)
            )
            ends, inner = jnp.exp(ends - top), jnp.exp(inner - top)
            total = jnp.sum(ends, axis=-1, keepdims=True) + jnp.sum(inner, axis=-1, keepdims=True)
            ends, inner = ends * (1.0 / total), inner * (1.0 / total)
            probs[2 * b + hp, :, 0:256] = ends
            probs[2 * b + hp, :, 256:] = inner
            mixed = dot_nn(spread(ends, inner), values).astype(BF)
            columns = pl.ds(pl.multiple_of(hp * 512, 512), 512)
            select[rows, columns] = jnp.concatenate([mixed[:256], mixed[256:]], axis=1)
            return carry

        lax.fori_loop(0, 2, pair_of_heads, 0)

    attend(0)
    attend(1)
    for n in FEED:
        gather_step(n, 3)
    def all_sent(numbers):
        for n in numbers:
            for copy in gather_sends[n] + passed[n]:
                copy.wait_send()
            if n % 3 == 0:
                for copy in direct_sends[n // 3]:
                    copy.wait_send()

    all_sent(ATTENTION)

    def second_norm(i, carry):
        rows = pl.ds(pl.multiple_of(i * 256, 256), 256)
        value = x_ref[rows].astype(F32) + dot_nn(select[rows], output_full[...])
        middle[rows] = value
        out[rows] = value
        second_cot[rows] = jnp.zeros((256, D), F32)
        normed = (value * inverse_rms(value) * feed_gain).astype(BF)
        pair_buffer[(0, 0, i) + (ALL,) * 5 + (slice(0, D),)] = normed.reshape((2,) * 4 + (16, D))
        return carry

    lax.fori_loop(0, 2, second_norm, 0)
    all_passed(FEED)
    all_sent(FEED)

    sum_sends, sum_steps, sum_directs = [], {}, {}

    def halve(number):
        if isinstance(number, int) and number >= 4:
            array, lead = 1, (ALL,) * 6
            columns = pl.ds(0, D) if number == 4 else pl.ds(D, HD)
        else:
            array, lead, columns = 0, (number // 2, number % 2) + (ALL,) * 4, ALL
        return remote(
            weights[array].at[lead + (1 - core, ALL, columns)],
            core_in[array].at[lead + (ALL, columns)],
            half_send.at[number],
            half_recv.at[number],
            peers[CORE],
        )

    def sum_send_step(n, step):
        array, first, count = PIECES[n][:3]
        order = order_of(PIECES[n])
        bit = order[step]
        source = tuple(
            mine[b] if b in order[:step] else (1 - mine[b] if b == bit else ALL) for b in range(6)
        )
        target = tuple(mine[b] if b in order[: step + 1] else ALL for b in range(6))
        tail = (ALL, pl.ds(first, count))
        copy = remote(
            weights[array].at[source + (core,) + tail],
            arrive[array].at[target + tail],
            sum_send.at[n, step],
            sum_recv.at[n, step],
            peers[bit],
        )
        copy.start()
        sum_sends.append(copy)
        sum_steps[n] = copy

    def add(into, other, free):
        turns = max(free - 3, 0)

        def some(i, carry):
            lead = tuple(i // 2 ** (turns - 1 - n) % 2 for n in range(turns))
            for index in itertools.product((0, 1), repeat=free - turns):
                into[lead + index] = into[lead + index] + other[lead + index]
            return carry

        if turns > 0:
            lax.fori_loop(0, 2**turns, some, 0)
        else:
            some(0, 0)

    def first_sums(numbers, halves):
        for number in halves:
            half_copies[number].wait_recv()
        for n in numbers:
            array, first, count = PIECES[n][:3]
            tail = (ALL, pl.ds(first, count))
            add(
                weights[array].at[(ALL,) * 6 + (core,) + tail],
                core_in[array].at[(ALL,) * 6 + tail],
                6,
            )
            sum_send_step(n, 0)

    def next_sums(numbers, step):
        for n in numbers:
            array, first, count = PIECES[n][:3]
            order = order_of(PIECES[n])
            bit = order[step]
            tail = (ALL, pl.ds(first, count))
            sum_steps[n].wait_recv()
            here = tuple(mine[b] if b in order[: step + 1] else ALL for b in range(6))
            there = tuple(1 - mine[b] if b == bit else v for b, v in enumerate(here))
            into, other = weights[array].at[here + (core,) + tail], arrive[array].at[there + tail]
            add(into, other, 5 - step)
            if step < 2:
                sum_send_step(n, step + 1)

    def flipped(bits):
        return tuple(1 - mine[b] if b in bits else mine[b] for b in range(6))

    def sum_direct(group):
        array, first, count, cube = GROUPS[group]
        tail = (ALL, pl.ds(first, count))
        sum_directs[group] = []
        for k, bits in enumerate(cube_bits[cube]):
            copy = remote(
                weights[array].at[flipped(bits) + (core,) + tail],
                arrive[array].at[mine[:6] + tail],
                last_send.at[group, k],
                last_recv.at[group, k],
                cube_peers[cube][k],
            )
            copy.start()
            sum_sends.append(copy)
            sum_directs[group].append(copy)

    def last_sums(group):
        array, first, count, cube = GROUPS[group]
        tail = (ALL, pl.ds(first, count))
        total = weights[array][mine[:6] + (core,) + tail].astype(F32)
        for k, bits in enumerate(cube_bits[cube]):
            sum_directs[group][k].wait_recv()
            total = total + arrive[array][flipped(bits) + tail].astype(F32)
        sums[array][:, pl.ds(first, count)] = total

    def feed(j, carry):
        gate_at, up_at, down_at = (
            (j // 2, j % 2) + (ALL,) * 6 + (slice(n * D, n * D + D),) for n in range(3)
        )
        gate_rows = feed_buffer[gate_at].reshape(512, D)
        up_rows = feed_buffer[up_at].reshape(512, D)
        down_rows = feed_buffer[down_at].reshape(512, D)
        second_low = pair_buffer[(0, 0) + (ALL,) * 6 + (slice(0, D),)].reshape(TOKENS, D)
        hidden, gate_cot, up_cot = [], [], []
        for part in range(2):
            tokens = slice(256 * part, 256 * part + 256)
            gate = dot_nt(second_low[tokens], gate_rows)
            up = dot_nt(second_low[tokens], up_rows)
            hidden_cot = dot_nt(cot[tokens], down_rows)
            square = gate * gate
            bend = jnp.tanh(GELU_RATE * gate * (1.0 + GELU_CUBE * square))
            half = 0.5 * (1.0 + bend)
            gelu = gate * half
            slope = half + 0.5 * gate * (1.0 - bend * bend) * (
                GELU_RATE * (1.0 + 3.0 * GELU_CUBE * square)
            )
            hidden.append((gelu * up).astype(BF))
            gate_cot.append((hidden_cot * up * slope).astype(BF))
            up_cot.append((hidden_cot * gelu).astype(BF))
            out[tokens] += dot_nn(hidden[part], down_rows)
            second_cot[tokens] += dot_nn(gate_cot[part], gate_rows) + dot_nn(up_cot[part], up_rows)
        hidden, gate_cot, up_cot = (
            jnp.concatenate(parts, axis=0) for parts in (hidden, gate_cot, up_cot)
        )
        shape = (2,) * 5 + (16, D)
        feed_buffer[down_at] = dot_tn(hidden, cot[...]).astype(BF).reshape(shape)
        feed_buffer[gate_at] = dot_tn(gate_cot, second_low).astype(BF).reshape(shape)
        feed_buffer[up_at] = dot_tn(up_cot, second_low).astype(BF).reshape(shape)
        halve(j).start()
        return carry

    lax.fori_loop(0, 4, feed, 0)
    half_copies = [halve(number) for number in range(6)]

    stores = [pltpu.make_async_copy(out, out_hbm, load_sems.at[2])]
    stores[0].start()

    def second_back(i, total):
        rows = pl.ds(pl.multiple_of(i * 128, 128), 128)
        value = middle[rows]
        rms = inverse_rms(value)
        direct = second_cot[rows]
        total = total + jnp.sum(direct * value * rms, axis=0, keepdims=True)
        scaled = direct * feed_gain
        inner = jnp.mean(value * scaled, axis=-1, keepdims=True)
        value = cot[rows].astype(F32) + rms * scaled - value * (rms * rms * rms * inner)
        middle[rows] = value
        x_prev[rows] = value.astype(BF)
        return total

    feed_gain_cot = lax.fori_loop(0, 4, second_back, jnp.zeros((1, D), F32))

    def output_back(head, carry):
        rows = head_rows(head)
        select[TOKENS : 2 * TOKENS, rows] = dot_nt(x_prev[...], output_full[rows]).astype(BF)
        output_full[rows] = dot_tn(select[0:TOKENS, rows], x_prev[...]).astype(BF)
        return carry

    lax.fori_loop(0, HQ, output_back, 0)
    window_cot[...] = jnp.zeros_like(window_cot)

    def attend_back(b):
        def pair_of_heads(hp, carry):
            heads, rows = pl.ds(2 * hp, 2), slice(256 * b, 256 * b + 256)
            span = slice(256 * b, 256 * b + 768)
            keys, values = window[span, 0:HD], window[span, HD:]
            columns = pl.ds(pl.multiple_of(hp * 512, 512), 512)
            below = slice(TOKENS + 256 * b, TOKENS + 256 * b + 256)
            given = select[below, columns]
            given = jnp.concatenate([given[:, :HD], given[:, HD:]], axis=0)
            ends, inner = probs[2 * b + hp, :, 0:256], probs[2 * b + hp, :, 256:]
            prob_cot = dot_nt(given, values)
            ends_cot = jnp.where(upper(), prob_cot[:, 0:256], prob_cot[:, 512:])
            inner_cot = prob_cot[:, 256:512]
            total = jnp.sum(ends_cot * ends, axis=-1, keepdims=True) + jnp.sum(
                inner_cot * inner, axis=-1, keepdims=True
            )
            score_low = spread(ends * (ends_cot - total), inner * (inner_cot - total))
            query_cot = (dot_nn(score_low, keys) * score_scale).astype(BF)
            select[below, columns] = jnp.concatenate([query_cot[:256], query_cot[256:]], axis=1)
            window_cot[span, 0:HD] += dot_tn(score_low, query[heads, rows].reshape(512, HD))
            window_cot[span, HD:] += dot_tn(spread(ends, inner), given)
            return carry

        lax.fori_loop(0, 2, pair_of_heads, 0)

    def send_back(half):
        rows = slice(256 * half, 256 * half + 256)
        window[rows, 0:HD] = (window_cot[rows, 0:HD] * score_scale).astype(BF)
        window[rows, HD:] = window_cot[rows, HD:].astype(BF)
        copy = remote(
            window.at[rows], back_in.at[rows], edge_send.at[1 + half], edge_recv.at[1 + half], before
        )
        copy.start()
        return copy

    attend_back(0)
    backs = [send_back(0)]
    attend_back(1)
    backs.append(send_back(1))
    first_sums(FEED, range(4))

    def query_back(head, carry):
        rows = head_rows(head)
        both = jnp.concatenate(
            [
                dot_tn(select[TOKENS : 2 * TOKENS, rows], low[...]).reshape(32, 8, D),
                output_full[rows].astype(F32).reshape(32, 8, D),
            ],
            axis=1,
        )
        pair_buffer[(head // 2, head % 2) + (ALL,) * 6 + (slice(0, D),)] = (
            both.astype(BF).reshape((2,) * 5 + (16, D))
        )
        return carry

    lax.fori_loop(0, HQ, query_back, 0)
    half_copies[4].start()

    def first_back(i, carry):
        rows = pl.ds(pl.multiple_of(i * 256, 256), 256)
        below = pl.ds(pl.multiple_of(TOKENS + i * 256, 256), 256)
        second_cot[rows] = dot_nn(select[below], query_full[...])
        return carry

    lax.fori_loop(0, 2, first_back, 0)
    again = pltpu.make_async_copy(select_hbm, select, load_sems.at[1])
    again.start()
    first_sums(PAIR, (4,))
    for copy in backs:
        copy.wait()
    returned = back_in[...].astype(F32)
    edge_low = jnp.concatenate(
        [
            window_cot[TOKENS:, 0:HD] * score_scale + returned[:, 0:HD],
            window_cot[TOKENS:, HD:] + returned[:, HD:],
        ],
        axis=1,
    ).astype(BF)
    window[TOKENS:] = edge_low
    key_value_grad = dot_tn(low[...], edge_low).astype(BF)

    def first_gain(i, total):
        rows = pl.ds(pl.multiple_of(i * 256, 256), 256)
        own_rows = pl.ds(pl.multiple_of(TOKENS + i * 256, 256), 256)
        direct = second_cot[rows] + dot_nt(window[own_rows], key_value_full[...])
        second_cot[rows] = direct
        value = x_ref[rows].astype(F32)
        return total + jnp.sum(direct * value * inverse_rms(value), axis=0, keepdims=True)

    attn_gain_cot = lax.fori_loop(0, 2, first_gain, jnp.zeros((1, D), F32))

    def as_columns(row):
        return dot_tn(jnp.broadcast_to(row, (8, D)), jnp.full((8, HD), 0.125, F32))

    gain_cots = as_columns(attn_gain_cot) * lane_mask[0].astype(F32) + as_columns(
        feed_gain_cot
    ) * lane_mask[1].astype(F32)
    again.wait()
    key_value_rows = dot_tn(select[0:D], key_value_grad)
    gain_cot_rows = dot_tn(select[D:], gain_cots.astype(BF))
    both = jnp.concatenate(
        [
            (key_value_rows[:, 0:HD] + gain_cot_rows).reshape(DEVICES, 8, HD),
            key_value_rows[:, HD:].reshape(DEVICES, 8, HD),
        ],
        axis=1,
    )
    pair_buffer[(ALL,) * 8 + (slice(D, D + HD),)] = both.astype(BF).reshape((2,) * 7 + (16, HD))
    half_copies[5].start()

    def input_back(i, carry):
        rows = pl.ds(pl.multiple_of(i * 128, 128), 128)
        value = x_ref[rows].astype(F32)
        rms = inverse_rms(value)
        scaled = second_cot[rows] * attn_gain
        inner = jnp.mean(value * scaled, axis=-1, keepdims=True)
        second_cot[rows] = middle[rows] + rms * scaled - value * (rms * rms * rms * inner)
        return carry

    lax.fori_loop(0, 4, input_back, 0)
    first_sums(SMALL, (5,))
    next_sums(FEED, 0)
    next_sums(PAIR, 0)
    stores.append(pltpu.make_async_copy(second_cot, input_grad_hbm, load_sems.at[3]))
    stores[1].start()
    next_sums(FEED, 1)
    next_sums(PAIR, 1)
    next_sums(SMALL, 0)
    next_sums(FEED, 2)
    sum_direct(2)
    sum_direct(3)
    next_sums(PAIR, 2)
    sum_direct(0)
    next_sums(SMALL, 1)
    next_sums(SMALL, 2)
    sum_direct(1)
    last_sums(2)
    last_sums(3)
    last_sums(0)
    last_sums(1)
    small = sums[1][:, D:]
    natural = lax.dot_general(
        small,
        turn[...].astype(F32),
        (((1,), (1,)), ((), ())),
        precision=lax.Precision.HIGHEST,
        preferred_element_type=F32,
    )
    gain_row = lax.broadcasted_iota(jnp.int32, (16, HD), 0) == 5
    sums[1][:, D:] = jnp.where(gain_row, small, natural)
    for copy in stores:
        copy.wait()

    now, outgo, result = wide.at[0:D], wide.at[D : D + 128], wide.at[D + 128 : D + 256]
    outgo[...] = jnp.zeros((128, D), F32)
    for n in range(3):
        outgo[16 * n : 16 * n + 16] = fresh_of(sums[0][:, n * D : n * D + D], moments[4 + n][...])
    outgo[48:56] = fresh_of(sums[1][0:8, 0:D], moments[0][...])
    outgo[72:80] = fresh_of(sums[1][8:16, 0:D], moments[3][...])
    outgo[80:85, 0:HD] = fresh_of(sums[1][0:5, D:], moments[1][...])
    outgo[96:101, 0:HD] = fresh_of(sums[1][8:13, D:], moments[2][...])
    rows_out[...] = outgo[...].astype(BF)
    group = mine[0] * 4 + mine[2] * 2 + mine[4]

    def far_group(bits):
        flipped = [1 - mine[bit] if bit in bits else mine[bit] for bit in FAR]
        return flipped[0] * 4 + flipped[1] * 2 + flipped[2]

    def sixteen(ref, number):
        return ref.at[pl.ds(pl.multiple_of(number * 16, 16), 16)]

    copies = []
    for n, bits in enumerate(far_bits):
        copy = remote(
            sixteen(rows_out, far_group(bits)),
            sixteen(rows_in, group),
            far_send.at[n],
            far_recv.at[n],
            far_peers[n],
        )
        copy.start()
        copies.append(copy)
    sixteen(rows_in, group)[...] = sixteen(rows_out, group)[...]
    for copy in copies:
        copy.wait_recv()
    rows = rows_in[...]

    def block_at(number):
        return (number // 8, number // 4 % 2, number // 2 % 2, number % 2)

    for r in range(5):
        strip = dot_tn(rows[:, 128 * r : 128 * r + 128], rows[:, 128 * r :])
        for number, (row, column) in enumerate(BLOCKS):
            if row == r:
                at = 128 * (column - r)
                blocks[block_at(number)] = strip[:, at : at + 128]
    blocks[block_at(15)] = jnp.zeros((128, 128), F32)
    near_mine = tuple(mine[bit] for bit in NEAR)

    def near_of(bits):
        return tuple(1 - mine[bit] if bit in bits else mine[bit] for bit in NEAR)

    halves = remote(
        blocks.at[1 - core], blocks_in, block_send.at[7], block_recv.at[7], peers[CORE]
    )
    halves.start()
    halves.wait()
    blocks[core] = blocks[core] + blocks_in[...]
    block_copies = []
    for n, bits in enumerate(near_bits):
        copy = remote(
            blocks.at[(core,) + near_of(bits)],
            blocks_arrive.at[near_mine],
            block_send.at[n],
            block_recv.at[n],
            near_peers[n],
        )
        copy.start()
        block_copies.append(copy)
    total = blocks[(core,) + near_mine]
    for copy in block_copies:
        copy.wait_recv()
    for n, bits in enumerate(near_bits):
        total = total + blocks_arrive[near_of(bits)]
    own_block = blocks_whole.at[(core,) + near_mine]
    own_block[...] = total
    whole_copies, whole_passed = [], []

    def whole_pass(n, part):
        copy = remote(
            part, part, whole_pass_send.at[n], whole_pass_recv.at[n], peers[CORE]
        )
        copy.start()
        whole_passed.append(copy)

    for n, bits in enumerate(near_bits):
        copy = remote(own_block, own_block, whole_send.at[n], whole_recv.at[n], near_peers[n])
        copy.start()
        whole_copies.append(copy)
    whole_pass(7, own_block)
    for n, bits in enumerate(near_bits):
        whole_copies[n].wait_recv()
        whole_pass(n, blocks_whole.at[(core,) + near_of(bits)])
    for copy in whole_passed:
        copy.wait_recv()
    square_sum = jnp.zeros((1, 1), F32)
    same = lax.broadcasted_iota(jnp.int32, (128, 128), 0) == lax.broadcasted_iota(
        jnp.int32, (128, 128), 1
    )
    for number, (row, column) in enumerate(BLOCKS):
        if row == column:
            diagonal = jnp.where(same, blocks_whole[block_at(number)], 0.0)
            square_sum = square_sum + jnp.sum(
                jnp.sum(diagonal, axis=0, keepdims=True), axis=1, keepdims=True
            )
    factor = 1.0 / (jnp.sqrt(square_sum) + ORTHO_EPS)
    for number, (row, column) in enumerate(BLOCKS):
        part = blocks_whole[block_at(number)] * (factor * factor)
        now[128 * row : 128 * row + 128, 128 * column : 128 * column + 128] = part
        if row != column:
            now[128 * column : 128 * column + 128, 128 * row : 128 * row + 128] = part.T
    result[...] = rows_in[...].astype(F32) * factor
    gram_high, gram_low = select.at[0:D, 0:D], select.at[D : 2 * D, 0:D]
    poly_high, poly_low = query_full.at[0:D], output_full.at[0:D]
    gram_high[...] = now[...].astype(BF)

    def iterate(_, carry):
        change = POLY_SECOND * now[...] + POLY_THIRD * dot_nn(gram_high[...], gram_high[...])
        poly_high[...] = change.astype(BF)
        result[...] = POLY_FIRST * result[...] + dot_nn(result[...].astype(BF), poly_high[...])
        product = POLY_FIRST * now[...] + dot_nn(gram_high[...], poly_high[...])
        gram_low[...] = product.astype(BF)
        later = POLY_FIRST * product + dot_nn(gram_low[...], poly_high[...])
        now[...] = later
        gram_high[...] = later.astype(BF)
        return carry

    lax.fori_loop(0, NS_ITERS - 2, iterate, 0)
    gram_value = now[...]
    change = POLY_SECOND * gram_value + POLY_THIRD * dot_nn(gram_high[...], gram_high[...])
    poly_high[...], poly_low[...] = parts_of(change)
    gram_low[...] = (gram_value - gram_high[...].astype(F32)).astype(BF)
    gram, poly = (gram_high[...], gram_low[...]), (poly_high[...], poly_low[...])
    value = POLY_FIRST * result[...] + dot_exact(result[...], poly)

    def times_next_gram(rows):
        rows = dot_exact(rows, gram)
        rows = POLY_FIRST * rows + dot_exact(rows, poly)
        return POLY_FIRST * rows + dot_exact(rows, poly)

    once = times_next_gram(value)
    for copy in copies:
        copy.wait_send()
    rows_out[...] = (
        POLY_FIRST * value + POLY_SECOND * once + POLY_THIRD * times_next_gram(once)
    ).astype(BF)
    copies = []
    for n, bits in enumerate(far_bits):
        copy = remote(
            sixteen(rows_out, far_group(bits)),
            ortho.at[group],
            back_send.at[n],
            back_recv.at[n],
            far_peers[n],
        )
        copy.start()
        copies.append(copy)
    ortho[group] = sixteen(rows_out, group)[...]
    for copy in copies:
        copy.wait()
    for copy in block_copies + whole_copies + whole_passed:
        copy.wait_send()
    for copy in half_copies:
        copy.wait_send()
    for copy in sum_sends:
        copy.wait_send()


def block_constants():
    swap = np.array([0, 1, 3, 2])
    position = np.arange(DEVICES).reshape(4, 4, 4, 2)[swap][:, swap][:, :, swap].reshape(DEVICES)
    select = np.zeros((2 * D, 8 * DEVICES), np.float32)
    lane_mask = np.zeros((2, D, HD), np.float32)
    for i in range(D):
        select[i, position[i // 5] * 8 + i % 5] = 1.0
        select[D + i, position[i // 5] * 8 + 5] = 1.0
        lane_mask[0, i, i % 5] = 1.0
        lane_mask[1, i, 128 + i % 5] = 1.0
    index = np.arange(HD).reshape(4, 4, 16)[swap][:, swap].reshape(HD)
    turn = np.eye(HD, dtype=np.float32)[:, index]
    return tuple(jnp.asarray(part, BF) for part in (select, lane_mask, turn))


def block(inputs, cotangent, masters, norm_gains, moments):
    select, lane_mask, turn = block_constants()
    vmem = pl.BlockSpec(memory_space=pltpu.VMEM)
    anywhere = pl.BlockSpec(memory_space=pl.ANY)
    dma = pltpu.SemaphoreType.DMA
    halves = [pltpu.VMEM((2,) * 6 + (16, width), BF) for width in WIDTHS]
    results = pl.pallas_call(
        block_kernel,
        out_shape=[jax.ShapeDtypeStruct((TOKENS, D), F32)] * 2
        + [jax.ShapeDtypeStruct((16, width), F32) for width in WIDTHS]
        + [jax.ShapeDtypeStruct((8, 16, D), BF)],
        in_specs=[vmem, anywhere] + [vmem] * 8 + [anywhere, vmem, vmem] + [vmem] * 7,
        out_specs=[anywhere] * 2 + [vmem] * 3,
        scratch_shapes=[pltpu.VMEM((2,) * 7 + (16, width), BF) for width in WIDTHS]
        + halves
        + halves
        + [pltpu.VMEM((16, width), BF) for width in WIDTHS]
        + [
            pltpu.VMEM((16, D), F32),
            pltpu.VMEM((16, HD), F32),
            pltpu.VMEM((TOKENS, D), BF),
            pltpu.VMEM((TOKENS, D), BF),
            pltpu.VMEM((2 * D, 8 * DEVICES), BF),
            pltpu.VMEM((TOKENS, D), BF),
            pltpu.VMEM((HQ * HD, D), BF),
            pltpu.VMEM((HQ * HD, D), BF),
            pltpu.VMEM((D, 2 * HD), BF),
            pltpu.VMEM((8, D), F32),
            pltpu.VMEM((HQ, TOKENS, HD), BF),
            pltpu.VMEM((2 * TOKENS, 2 * HD), BF),
            pltpu.VMEM((4, 512, 512), F32),
            pltpu.VMEM((3 * TOKENS, D), F32),
            pltpu.VMEM((2 * TOKENS, 2 * HD), F32),
            pltpu.VMEM((TOKENS, 2 * HD), BF),
            pltpu.VMEM((2, 2, 2, 2, 128, 128), F32),
            pltpu.VMEM((2, 2, 2, 128, 128), F32),
            pltpu.VMEM((2, 2, 2, 128, 128), F32),
            pltpu.VMEM((2, 2, 2, 2, 128, 128), F32),
            pltpu.VMEM((128, D), BF),
            pltpu.VMEM((128, D), BF),
            dma((4,)),
            dma((2,)),
            dma((COUNT, 3)),
            dma((COUNT, 3)),
            dma((COUNT, 3)),
            dma((COUNT, 3)),
            dma((6,)),
            dma((6,)),
            dma((COUNT, 3)),
            dma((COUNT, 3)),
            dma((4, 7)),
            dma((4, 7)),
            dma((4, 7)),
            dma((4, 7)),
            dma((3,)),
            dma((3,)),
            dma((7,)),
            dma((7,)),
            dma((8,)),
            dma((8,)),
            dma((7,)),
            dma((7,)),
            dma((8,)),
            dma((8,)),
            dma((7,)),
            dma((7,)),
        ],
        compiler_params=pltpu.CompilerParams(
            collective_id=0, has_side_effects=True, vmem_limit_bytes=59 * 2**20
        ),
        name="block",
    )(inputs, cotangent, *masters, norm_gains, select, lane_mask, turn, *moments)
    return results[0:2], results[2:4], results[4]


SIZES = ((D, HQ * HD), (D, HD), (D, HD), (HQ * HD, D), (D, FF), (D, FF), (FF, D))


def finish_kernel(*refs):
    feed, rest, ortho = refs[:3]
    moments, masters, gains, large = refs[3:10], refs[10:17], refs[17:20], refs[20:22]
    grad_outs, moment_outs, master_outs, gain_outs, large_outs = (
        refs[22:29],
        refs[29:36],
        refs[36:43],
        refs[43:47],
        refs[47:49],
    )
    held, sems = refs[49:51]
    copies = [
        pltpu.make_async_copy(large[n], held.at[n], sems.at[n]) for n in range(2)
    ]
    for copy in copies:
        copy.start()
    stores = []
    for n in range(2):
        copies[n].wait()
        stores.append(pltpu.make_async_copy(held.at[n], large_outs[n], sems.at[2 + n]))
        stores[n].start()
    own = (
        rest[0:8, 0:D],
        rest[0:5, D:],
        rest[8:13, D:],
        rest[8:16, 0:D],
        feed[:, 0:D],
        feed[:, D : 2 * D],
        feed[:, 2 * D :],
    )
    turned = tuple(ortho[n].astype(F32) for n in range(7))
    turned = (
        turned[3][0:8],
        turned[5][0:5, 0:HD],
        turned[6][0:5, 0:HD],
        turned[4][8:16],
        turned[0],
        turned[1],
        turned[2],
    )
    for n in range(7):
        rows, columns = SIZES[n]
        ratio = math.sqrt(max(rows, columns) / rows)
        grad_outs[n][...] = own[n]
        moment_outs[n][...] = fresh_of(own[n], moments[n][...])
        master_outs[n][...] = (
            masters[n][...] * (1.0 - MUON_RATE * MUON_DECAY) - MUON_RATE * ratio * turned[n]
        )
    gain_grads = jnp.concatenate([rest[5:6, D : D + 5], rest[5:6, D + 128 : D + 133]], axis=0)
    norm_gains, gain_first, gain_second = (ref[...] for ref in gains)
    first_moments = BETA_FIRST * gain_first + (1.0 - BETA_FIRST) * gain_grads
    second_moments = BETA_SECOND * gain_second + (1.0 - BETA_SECOND) * gain_grads * gain_grads
    first_hat = first_moments / (1.0 - BETA_FIRST**ADAM_STEP)
    second_hat = second_moments / (1.0 - BETA_SECOND**ADAM_STEP)
    gain_outs[0][...] = gain_grads
    gain_outs[1][...] = first_moments
    gain_outs[2][...] = second_moments
    gain_outs[3][...] = norm_gains - ADAM_RATE * first_hat / (jnp.sqrt(second_hat) + ADAM_EPS)
    for copy in stores:
        copy.wait()


def finish(grads, ortho, moments, masters, gains, large):
    shapes = [jax.ShapeDtypeStruct(moment.shape, F32) for moment in moments]
    vmem = pl.BlockSpec(memory_space=pltpu.VMEM)
    anywhere = pl.BlockSpec(memory_space=pl.ANY)
    return pl.pallas_call(
        finish_kernel,
        out_shape=shapes * 3
        + [jax.ShapeDtypeStruct((2, 5), F32)] * 4
        + [jax.ShapeDtypeStruct((TOKENS, D), F32)] * 2,
        in_specs=[vmem] * 20 + [anywhere] * 2,
        out_specs=[vmem] * 25 + [anywhere] * 2,
        scratch_shapes=[pltpu.VMEM((2, TOKENS, D), F32), pltpu.SemaphoreType.DMA((4,))],
        name="finish",
    )(*grads, ortho, *moments, *masters, *gains, *large)


def body(
    inputs,
    cotangent,
    query_weight,
    key_weight,
    value_weight,
    output_weight,
    gate_weight,
    up_weight,
    down_weight,
    norm_gains,
    query_moment,
    key_moment,
    value_moment,
    output_moment,
    gate_moment,
    up_moment,
    down_moment,
    gain_first,
    gain_second,
):
    moments = (
        query_moment.T,
        key_moment,
        value_moment,
        output_moment,
        gate_moment.T,
        up_moment.T,
        down_moment,
    )
    masters = (
        query_weight.T,
        key_weight,
        value_weight,
        output_weight,
        gate_weight.T,
        up_weight.T,
        down_weight,
    )
    large, grads, ortho = block(inputs, cotangent, masters, norm_gains, moments)
    outs = finish(grads, ortho, moments, masters, (norm_gains, gain_first, gain_second), large)

    def natural(seven):
        return tuple(part.T if n in (0, 4, 5) else part for n, part in enumerate(seven))

    return (
        tuple(outs[25:27])
        + natural(outs[0:7])
        + natural(outs[7:14])
        + natural(outs[14:21])
        + tuple(outs[21:25])
    )


def solution(mesh):
    rows, columns = P(AXES, None), P(None, AXES)
    seven = (columns, rows, rows, rows, columns, columns, rows)
    return jax.shard_map(
        body,
        mesh=mesh,
        in_specs=(rows, rows) + seven + (columns,) + seven + (columns, columns),
        out_specs=(rows, rows) + seven * 3 + (columns,) * 4,
        check_vma=False,
    )
```
